256 devices in a mesh: row: 8 (over y, core), col: 32 (over x, z).
Axes of the slice: x: 4, y: 4, z: 8, core: 2. Of those that a mesh axis runs over, the one named last changes fastest.
Arguments:
- initial_warmth: float32 [128, 512, 128], P('row', 'col'), may hold values from -3.5 to 3.5
- substance_factor: float32 [128, 512, 128], P('row', 'col'), may hold values from 1 to 4
Outputs:
- new_temperature: float32 [128, 512, 128], P('row', 'col')
The draws below stay inside these ranges and needn't reach their ends.
All inputs are finite; a program needn't handle non-finite values.
Results may differ from the reference program's by a relative error of at most 0.00075.
Values sent between devices are 32-bit elements; how exact they have to be, the bound alone decides.
A program may use at most 128 MiB of HBM per device.

```python
import math
import jax
import jax.numpy as jnp
from jax import lax

NZ = 128
NX = 128
NY = 512


def draw_initial_warmth(key, part):
    rough = jax.random.normal(key, (NX, NY, NZ), jnp.float32)
    rough = jnp.clip(rough, -3.5, 3.5)
    return rough


def levels(own_key, dims, shards, smallest, largest):
    def one(position, parts):
        steps = jax.random.uniform(jax.random.fold_in(jax.random.fold_in(own_key, 6), position), (parts,), jnp.float32, smallest / len(shards), largest / len(shards))
        return jnp.repeat(jnp.exp(steps), dims[position] // parts).reshape((-1,) + (1,) * (len(dims) - position - 1))

    gain = one(*shards[0])
    for cut in shards[1:]:
        gain = gain * one(*cut)
    return gain


def setup_inputs(seed: int = 0) -> dict:
    keys = jax.random.split(jax.random.key(seed), 3)
    return {
        "initial_warmth": draw_initial_warmth(jax.random.fold_in(keys[2], 71), 0),
        "substance_factor": jnp.clip(jnp.exp(math.log(4.0) - 1.3862944 * jax.random.uniform(keys[1], (NX, NY, NZ), jnp.float32) ** levels(keys[1], (NX, NY, NZ), ((0, 8), (1, 32)), -0.2, 0.2)), 1.0, 4.0),
    }


lateral = 1500.0
upright_direction = 2.0
warmed_wall_value = 0.5
chilled_wall_value = -0.5
warmth_responsiveness = 0.4

def harmonic(one_side, other_side):
    return 2.0 * one_side * other_side / (one_side + other_side)

def all_faces(diffusivity_scale, dimension, walls):
    length = diffusivity_scale.shape[dimension]
    inner = harmonic(lax.slice_in_dim(diffusivity_scale, 0, length - 1, axis=dimension), lax.slice_in_dim(diffusivity_scale, 1, length, axis=dimension))
    first_cell = lax.slice_in_dim(diffusivity_scale, 0, 1, axis=dimension)
    last_cell = lax.slice_in_dim(diffusivity_scale, length - 1, length, axis=dimension)
    if not walls:
        first_cell = jnp.zeros_like(first_cell)
        last_cell = jnp.zeros_like(last_cell)
    return jnp.concatenate([first_cell, inner, last_cell], axis=dimension)

def energy_current(field, faces, dimension, below, above):
    length = field.shape[dimension]
    edge_cell = lax.slice_in_dim(field, 0, 1, axis=dimension)
    prev_cells = jnp.concatenate([jnp.full_like(edge_cell, below), lax.slice_in_dim(field, 0, length - 1, axis=dimension)], axis=dimension)
    next_cells = jnp.concatenate([lax.slice_in_dim(field, 1, length, axis=dimension), jnp.full_like(edge_cell, above)], axis=dimension)
    plus_faces = lax.slice_in_dim(faces, 1, length + 1, axis=dimension)
    minus_faces = lax.slice_in_dim(faces, 0, length, axis=dimension)
    return plus_faces * (next_cells - field) - minus_faces * (field - prev_cells)

def implicit(side, faces, dimension, coefficient):
    length = side.shape[dimension]
    minus_faces = lax.slice_in_dim(faces, 0, length, axis=dimension)
    plus_faces = lax.slice_in_dim(faces, 1, length + 1, axis=dimension)
    low_band = jnp.moveaxis(-coefficient * minus_faces, dimension, -1)
    high_band = jnp.moveaxis(-coefficient * plus_faces, dimension, -1)
    main_band = jnp.moveaxis(1.0 + coefficient * (minus_faces + plus_faces), dimension, -1)
    low_band = low_band.at[..., 0].set(0.0)
    high_band = high_band.at[..., -1].set(0.0)
    moved_side = jnp.moveaxis(side, dimension, -1)[..., None]
    solved = lax.linalg.tridiagonal_solve(low_band, main_band, high_band, moved_side)[..., 0]
    return jnp.moveaxis(solved, -1, dimension)

def reference(initial_warmth, substance_factor):
    diffusivity_scale = substance_factor * (1.0 + warmth_responsiveness * jnp.tanh(initial_warmth))
    crosswise_interfaces = all_faces(diffusivity_scale, 0, False)
    spanwise_interfaces = all_faces(diffusivity_scale, 1, False)
    gravity_interfaces = all_faces(diffusivity_scale, 2, True)
    energy_current_crosswise = energy_current(initial_warmth, crosswise_interfaces, 0, 0.0, 0.0)
    energy_current_spanwise = energy_current(initial_warmth, spanwise_interfaces, 1, 0.0, 0.0)
    energy_current_gravity = energy_current(initial_warmth, gravity_interfaces, 2, warmed_wall_value, chilled_wall_value)
    explicit_rhs = 2.0 * (lateral * energy_current_crosswise + lateral * energy_current_spanwise + upright_direction * energy_current_gravity)
    first_section = implicit(explicit_rhs, gravity_interfaces, 2, upright_direction)
    second_section = implicit(first_section, spanwise_interfaces, 1, lateral)
    closing_portion = implicit(second_section, crosswise_interfaces, 0, lateral)
    return initial_warmth + closing_portion
```

```python
import functools

import jax
import jax.numpy as jnp
from jax import lax
from jax.experimental import pallas as pl
from jax.experimental.pallas import tpu as pltpu
from jax.sharding import PartitionSpec as P

MESH = pl.DeviceIdType.MESH
LATERAL = 1500.0
UPRIGHT = 2.0
WARM_WALL = 0.5
CHILL_WALL = -0.5
RESPONSE = 0.4
B = 16
NZ = 128
ROWS = 8
GROUP = 8
GROUPS = 4
STEPS = (1, 2, 4, 8, 16, 32, 64)


def inverse(value):
    guess = pl.reciprocal(value, approx=True)
    return guess * (2.0 - value * guess)


def conductivity(temperature, factor):
    return factor * (1.0 + RESPONSE * jnp.tanh(temperature))


def half_resistance(conduct):
    return inverse((2.0 * LATERAL) * conduct)


def block_coefficients(half, link, back, green_first, green_last, out):
    left = jnp.ones((B, NZ), jnp.float32)
    right = jnp.ones((B, NZ), jnp.float32)
    lefts, rights = {}, {}
    for step in range(1, B):
        i, j = step, B - step
        resist = half[i - 1] + half[i]
        lefts[i] = inverse(1.0 + left * resist)
        link[i] = lefts[i]
        back[i] = lefts[i] * resist
        left = 1.0 + left * lefts[i]
        resist = half[j - 1] + half[j]
        rights[j] = inverse(1.0 + right * resist)
        right = 1.0 + right * rights[j]
    first, last = inverse(right), inverse(left)
    out[0] = first + half[0]
    out[1] = last + half[B - 1]
    green_first[0] = first
    green_last[B - 1] = last
    for i in range(1, B):
        first = first * rights[i]
        green_first[i] = first
        last = last * lefts[B - i]
        green_last[B - 1 - i] = last
    out[2] = first


def block_ends(load, green_first, green_last, out):
    firsts = [None] * 4
    lasts = [None] * 4
    for i in range(B):
        value = load(i)
        a, b = green_first[i] * value, green_last[i] * value
        k = i % 4
        firsts[k] = a if firsts[k] is None else firsts[k] + a
        lasts[k] = b if lasts[k] is None else lasts[k] + b
    out[0] = (firsts[0] + firsts[1]) + (firsts[2] + firsts[3])
    out[1] = (lasts[0] + lasts[1]) + (lasts[2] + lasts[3])


def block_solve(load, store, link, back, green_last):
    values = [load(0)]
    for i in range(1, B):
        values.append(load(i) + link[i] * values[-1])
    solved = values[-1] * green_last[B - 1]
    store(B - 1, solved)
    for i in range(B - 1, 0, -1):
        solved = back[i] * values[i - 1] + link[i] * solved
        store(i - 1, solved)


def chain_factors(count, coeffs, link, inv, carry):
    previous = None
    for i in range(1, count):
        pivot = coeffs[i - 1, 1] + coeffs[i, 0]
        if previous is not None:
            link[i] = coeffs[i - 1, 2] * previous
            pivot = pivot - coeffs[i - 1, 2] * link[i]
        previous = inverse(pivot)
        inv[i] = previous
        carry[i] = coeffs[i, 2] * previous


def chain_solve(count, ends, link, inv, carry, out):
    values = [None, ends[1, 0] - ends[0, 1]]
    for i in range(2, count):
        values.append((ends[i, 0] - ends[i - 1, 1]) + link[i] * values[-1])
    flux = values[count - 1] * inv[count - 1]
    out[count - 1] = flux
    for i in range(count - 2, 0, -1):
        flux = values[i] * inv[i] + carry[i] * flux
        out[i] = flux


def group_coefficients(coeffs, link, inv, carry, from_left, from_right, out):
    n = GROUP
    zero = jnp.zeros((B, NZ), jnp.float32)
    one = jnp.ones((B, NZ), jnp.float32)
    flux = carry[n - 1]
    from_right[n] = one
    from_right[0] = zero
    from_right[n - 1] = flux
    out[1] = coeffs[n - 1, 1] - coeffs[n - 1, 2] * flux
    for i in range(n - 2, 0, -1):
        flux = carry[i] * flux
        from_right[i] = flux
    out[2] = coeffs[0, 2] * flux
    values = [None, coeffs[0, 2]]
    for i in range(2, n):
        values.append(link[i] * values[-1])
    flux = values[n - 1] * inv[n - 1]
    from_left[0] = one
    from_left[n] = zero
    from_left[n - 1] = flux
    for i in range(n - 2, 0, -1):
        flux = values[i] * inv[i] + carry[i] * flux
        from_left[i] = flux
    out[0] = coeffs[0, 0] - coeffs[0, 2] * flux


def up(value, stride):
    return pltpu.roll(value, stride, axis=1)


def down(value, stride):
    return pltpu.roll(value, NZ - stride, axis=1)


def upright_bands(conduct, lane):
    below = up(conduct, 1)
    face = (2.0 * conduct * below) * inverse(conduct + below)
    inner = jnp.where(lane == 0, 0.0, UPRIGHT * face)
    wall = jnp.where((lane == 0) | (lane == NZ - 1), UPRIGHT * conduct, 0.0)
    main = 1.0 + inner + down(inner, 1) + wall
    return inner, main


def upright_step(link, main, stride):
    inv = inverse(main)
    low = link * up(inv, stride)
    high = link * inv
    new_main = main - low * link - down(high * link, stride)
    return low, high, low * up(link, stride), new_main


def kernel(
    warmth_hbm,
    factor_hbm,
    out_ref,
    warmth,
    factor,
    half_x,
    warmth_t,
    conduct_t,
    half_y,
    side_t,
    side_n,
    halo,
    low_f,
    high_f,
    scale_f,
    link_x,
    back_x,
    gf_x,
    gl_x,
    link_y,
    back_y,
    gf_y,
    gl_y,
    solved,
    co_z,
    co_x,
    co_r,
    end_z,
    end_x,
    end_r,
    ch_link,
    ch_inv,
    ch_carry,
    flux_z,
    flux_x,
    flux_r,
    from_left,
    from_right,
    load_sem,
    send_sem,
    recv_sem,
):
    row = lax.axis_index("row")
    col = lax.axis_index("col")
    me_x = col // GROUP
    me_z = lax.rem(col, GROUP)
    base = me_x * GROUP

    far_first = (4, 3, 5, 2, 6, 1, 7)
    z_peers = [(row, base + lax.rem(me_z + k, GROUP)) for k in far_first]
    x_peers = [(row, lax.rem(col + GROUP * k, GROUP * GROUPS)) for k in (2, 1, 3)]
    row_peers = [(lax.rem(row + k, ROWS), col) for k in far_first]
    columns = GROUP * GROUPS
    row_up, row_down = (lax.rem(row + 1, ROWS), col), (lax.rem(row + ROWS - 1, ROWS), col)
    col_up, col_down = (row, lax.rem(col + 1, columns)), (row, lax.rem(col + columns - 1, columns))

    barrier = pltpu.get_barrier_semaphore()
    everyone = [col_up, col_down] + row_peers + z_peers + x_peers
    for peer in everyone:
        pl.semaphore_signal(barrier, inc=1, device_id=peer, device_id_type=MESH)
    load_w = pltpu.make_async_copy(warmth_hbm, warmth, load_sem.at[0])
    load_f = pltpu.make_async_copy(factor_hbm, factor, load_sem.at[1])
    load_w.start()
    load_f.start()
    pl.semaphore_wait(barrier, len(everyone))

    def remote(src, dst, which, peer):
        return pltpu.make_async_remote_copy(
            src_ref=src,
            dst_ref=dst,
            send_sem=send_sem.at[which],
            recv_sem=recv_sem.at[which],
            device_id=peer,
            device_id_type=MESH,
        )

    for k, array in enumerate((warmth_hbm, factor_hbm)):
        remote(array.at[:, B - 1, :], halo.at[4 + k], 0, col_up).start()
        remote(array.at[:, 0, :], halo.at[6 + k], 0, col_down).start()
        remote(array.at[B - 1], halo.at[k], 0, row_up).start()
        remote(array.at[0], halo.at[2 + k], 0, row_down).start()

    def settle(buffer, count, sem):
        view = buffer.at[pl.ds(0, count)]
        pltpu.make_async_copy(view, view, sem).wait()

    def spread(buffer, index, which, peers):
        for peer in peers:
            remote(buffer.at[index], buffer.at[index], which, peer).start()

    load_w.wait()
    load_f.wait()

    before = None
    for i in range(B):
        w = warmth[i]
        c = conductivity(w, factor[i])
        h = half_resistance(c)
        half_x[i] = h
        warmth_t[pl.ds(i, B, stride=B), :] = w
        conduct_t[pl.ds(i, B, stride=B), :] = c
        half_y[pl.ds(i, B, stride=B), :] = h
        if before is None:
            edge_low_c = c
            flux_low = None
        else:
            flux_high = inverse(before[1] + h) * (w - before[0])
            gain = flux_high if flux_low is None else flux_high - flux_low
            side_t[pl.ds(i - 1, B, stride=B), :] = gain
            flux_low = flux_high
        before = (w, h)
    side_t[pl.ds(B - 1, B, stride=B), :] = -flux_low
    edge_high_c = c

    class Rows:
        def __init__(self, ref):
            self.ref = ref

        def __getitem__(self, i):
            return self.ref[i * B : (i + 1) * B, :]

    half_rows = Rows(half_y)
    block_coefficients(half_rows, link_y, back_y, gf_y, gl_y, co_z.at[me_z])
    spread(co_z, me_z, 1, z_peers)

    flux_low = None
    for i in range(B):
        if i < B - 1:
            flux_high = inverse(half_rows[i] + half_rows[i + 1]) * (
                warmth_t[(i + 1) * B : (i + 2) * B, :] - warmth_t[i * B : (i + 1) * B, :]
            )
        gain = flux_high if i == 0 else (-flux_low if i == B - 1 else flux_high - flux_low)
        side_t[i * B : (i + 1) * B, :] = side_t[i * B : (i + 1) * B, :] + gain
        flux_low = flux_high

    lane = lax.broadcasted_iota(jnp.int32, (64, NZ), 1)

    def upright(n, carry):
        rows = pl.ds(pl.multiple_of(n * 64, 64), 64)
        w = warmth_t[rows, :]
        c = conduct_t[rows, :]
        link, main = upright_bands(c, lane)
        lower = UPRIGHT * c * (w - WARM_WALL)
        flux = jnp.where(lane == 0, lower, link * (w - up(w, 1)))
        upper = UPRIGHT * c * (CHILL_WALL - w)
        flux_above = jnp.where(lane == NZ - 1, upper, down(flux, 1))
        side = 2.0 * (side_t[rows, :] + (flux_above - flux))
        for stride in STEPS:
            low, high, link, main = upright_step(link, main, stride)
            side = side + low * up(side, stride) + down(high * side, stride)
        side_t[rows, :] = side * inverse(main)
        return carry

    lax.fori_loop(0, 4, upright, 0)

    last = B * (B - 1)
    edge_c = jnp.concatenate(
        [edge_low_c, edge_high_c, conduct_t[0:B, :], conduct_t[last : last + B, :]], axis=0
    )
    link, main = upright_bands(edge_c, lane)
    for n, stride in enumerate(STEPS):
        low, high, link, main = upright_step(link, main, stride)
        low_f[n] = low
        high_f[n] = high
    scale_f[...] = inverse(main)

    settle(halo, 8, recv_sem.at[0])

    def through(near_w, near_h, k, present):
        other = halo[k]
        resist = near_h + half_resistance(conductivity(other, halo[k + 1]))
        return (2.0 * present) * (inverse(resist) * (other - near_w))

    def flag(condition):
        return jnp.where(condition, 1.0, 0.0).astype(jnp.float32)

    share = jnp.concatenate(
        [
            through(warmth[0], half_x[0], 0, flag(row > 0)),
            through(warmth[B - 1], half_x[B - 1], 2, flag(row < ROWS - 1)),
            through(warmth_t[0:B, :], half_rows[0], 4, flag(col > 0)),
            through(warmth_t[last : last + B, :], half_rows[B - 1], 6, flag(col < columns - 1)),
        ],
        axis=0,
    )
    for n, stride in enumerate(STEPS):
        share = share + low_f[n] * up(share, stride) + down(high_f[n] * share, stride)
    share = share * scale_f[...]
    side_t[0:B, :] = side_t[0:B, :] + share[2 * B : 3 * B]
    side_t[last : last + B, :] = side_t[last : last + B, :] + share[3 * B : 4 * B]
    side_t[pl.ds(0, B, stride=B), :] = side_t[pl.ds(0, B, stride=B), :] + share[0:B]
    side_t[pl.ds(B - 1, B, stride=B), :] = side_t[pl.ds(B - 1, B, stride=B), :] + share[B : 2 * B]

    side_rows = Rows(side_t)
    block_ends(lambda i: side_rows[i], gf_y, gl_y, end_z.at[me_z])
    spread(end_z, me_z, 2, z_peers)

    settle(co_z, GROUP - 1, recv_sem.at[1])
    chain_factors(GROUP, co_z, ch_link.at[0], ch_inv.at[0], ch_carry.at[0])
    group_coefficients(
        co_z, ch_link.at[0], ch_inv.at[0], ch_carry.at[0], from_left, from_right, co_x.at[me_x]
    )
    spread(co_x, me_x, 3, x_peers)
    block_coefficients(half_x, link_x, back_x, gf_x, gl_x, co_r.at[row])
    spread(co_r, row, 4, row_peers)

    def keep(i, value):
        solved[i] = value

    block_solve(lambda i: side_rows[i], keep, link_y, back_y, gl_y)
    zero = jnp.zeros((B, NZ), jnp.float32)
    for ref, count in ((flux_z, GROUP), (flux_x, GROUPS), (flux_r, ROWS)):
        ref[0] = zero
        ref[count] = zero

    settle(end_z, GROUP - 1, recv_sem.at[2])
    chain_solve(GROUP, end_z, ch_link.at[0], ch_inv.at[0], ch_carry.at[0], flux_z)
    end_x[me_x, 0] = end_z[0, 0] + co_z[0, 2] * flux_z[1]
    end_x[me_x, 1] = end_z[GROUP - 1, 1] - co_z[GROUP - 1, 2] * flux_z[GROUP - 1]
    spread(end_x, me_x, 5, x_peers)

    settle(co_x, GROUPS - 1, recv_sem.at[3])
    chain_factors(GROUPS, co_x, ch_link.at[1], ch_inv.at[1], ch_carry.at[1])
    settle(co_r, ROWS - 1, recv_sem.at[4])
    chain_factors(ROWS, co_r, ch_link.at[2], ch_inv.at[2], ch_carry.at[2])

    settle(end_x, GROUPS - 1, recv_sem.at[5])
    chain_solve(GROUPS, end_x, ch_link.at[1], ch_inv.at[1], ch_carry.at[1], flux_x)
    outer_low, outer_high = flux_x[me_x], flux_x[me_x + 1]

    def inner_flux(i):
        return flux_z[i] + from_left[i] * outer_low + from_right[i] * outer_high

    flux_low, flux_high = inner_flux(me_z), inner_flux(me_z + 1)
    for i in range(B):
        side_n[pl.ds(i, B, stride=B), :] = solved[i] - gf_y[i] * flux_low + gl_y[i] * flux_high

    section = Rows(side_n)
    block_ends(lambda i: section[i], gf_x, gl_x, end_r.at[row])
    spread(end_r, row, 6, row_peers)
    block_solve(lambda i: section[i], keep, link_x, back_x, gl_x)

    settle(end_r, ROWS - 1, recv_sem.at[6])
    chain_solve(ROWS, end_r, ch_link.at[2], ch_inv.at[2], ch_carry.at[2], flux_r)
    flux_low, flux_high = flux_r[row], flux_r[row + 1]
    for i in range(B):
        out_ref[i] = warmth[i] + (solved[i] - gf_x[i] * flux_low + gl_x[i] * flux_high)

    settle(halo, 8, send_sem.at[0])
    settle(co_z, GROUP - 1, send_sem.at[1])
    settle(end_z, GROUP - 1, send_sem.at[2])
    settle(co_x, GROUPS - 1, send_sem.at[3])
    settle(co_r, ROWS - 1, send_sem.at[4])
    settle(end_x, GROUPS - 1, send_sem.at[5])
    settle(end_r, ROWS - 1, send_sem.at[6])


def shards(warmth, factor):
    def vmem(*shape):
        return pltpu.VMEM(shape, jnp.float32)

    scratch = [
        vmem(B, B, NZ),
        vmem(B, B, NZ),
        vmem(B, B, NZ),
        vmem(B * B, NZ),
        vmem(B * B, NZ),
        vmem(B * B, NZ),
        vmem(B * B, NZ),
        vmem(B * B, NZ),
        vmem(8, B, NZ),
        vmem(len(STEPS), 4 * B, NZ),
        vmem(len(STEPS), 4 * B, NZ),
        vmem(4 * B, NZ),
    ]
    scratch += [vmem(B, B, NZ) for _ in range(8)]
    scratch += [
        vmem(B, B, NZ),
        vmem(GROUP, 3, B, NZ),
        vmem(GROUPS, 3, B, NZ),
        vmem(ROWS, 3, B, NZ),
        vmem(GROUP, 2, B, NZ),
        vmem(GROUPS, 2, B, NZ),
        vmem(ROWS, 2, B, NZ),
        vmem(3, GROUP, B, NZ),
        vmem(3, GROUP, B, NZ),
        vmem(3, GROUP, B, NZ),
        vmem(GROUP + 1, B, NZ),
        vmem(GROUPS + 1, B, NZ),
        vmem(ROWS + 1, B, NZ),
        vmem(GROUP + 1, B, NZ),
        vmem(GROUP + 1, B, NZ),
        pltpu.SemaphoreType.DMA((2,)),
        pltpu.SemaphoreType.DMA((7,)),
        pltpu.SemaphoreType.DMA((7,)),
    ]
    return pl.pallas_call(
        kernel,
        out_shape=jax.ShapeDtypeStruct((B, B, NZ), jnp.float32),
        in_specs=[pl.BlockSpec(memory_space=pl.ANY)] * 2,
        out_specs=pl.BlockSpec(memory_space=pltpu.VMEM),
        scratch_shapes=scratch,
        compiler_params=pltpu.CompilerParams(
            collective_id=0, has_side_effects=True, vmem_limit_bytes=48 * 2**20
        ),
    )(warmth, factor)


def solution(mesh):
    return jax.shard_map(
        shards,
        mesh=mesh,
        in_specs=(P("row", "col", None), P("row", "col", None)),
        out_specs=P("row", "col", None),
        check_vma=False,
    )
```

```python
import functools

import jax
import jax.numpy as jnp
from jax import lax
from jax.experimental import pallas as pl
from jax.experimental.pallas import tpu as pltpu
from jax.sharding import PartitionSpec as P

MESH = pl.DeviceIdType.MESH
LATERAL = 1500.0
UPRIGHT = 2.0
WARM_WALL = 0.5
CHILL_WALL = -0.5
RESPONSE = 0.4
B = 16
NZ = 128
ROWS = 8
GROUP = 8
GROUPS = 4
STEPS = (1, 2, 4, 8, 16, 32, 64)
WEIGHTS = 19


def inverse(value):
    guess = pl.reciprocal(value, approx=True)
    return guess * (2.0 - value * guess)


def conductivity(temperature, factor):
    return factor * (1.0 + RESPONSE * jnp.tanh(temperature))


def half_resistance(conduct):
    return inverse((2.0 * LATERAL) * conduct)


def block_coefficients(half, link, back, green_first, green_last, out):
    left = jnp.ones((B, NZ), jnp.float32)
    right = jnp.ones((B, NZ), jnp.float32)
    lefts, rights = {}, {}
    for step in range(1, B):
        i, j = step, B - step
        resist = half[i - 1] + half[i]
        lefts[i] = inverse(1.0 + left * resist)
        link[i] = lefts[i]
        back[i] = lefts[i] * resist
        left = 1.0 + left * lefts[i]
        resist = half[j - 1] + half[j]
        rights[j] = inverse(1.0 + right * resist)
        right = 1.0 + right * rights[j]
    first, last = inverse(right), inverse(left)
    out[0] = first + half[0]
    out[1] = last + half[B - 1]
    green_first[0] = first
    green_last[B - 1] = last
    for i in range(1, B):
        first = first * rights[i]
        green_first[i] = first
        last = last * lefts[B - i]
        green_last[B - 1 - i] = last
    out[2] = first


def block_ends(load, green_first, green_last, out):
    firsts = [None] * 4
    lasts = [None] * 4
    for i in range(B):
        value = load(i)
        a, b = green_first[i] * value, green_last[i] * value
        k = i % 4
        firsts[k] = a if firsts[k] is None else firsts[k] + a
        lasts[k] = b if lasts[k] is None else lasts[k] + b
    out[0] = (firsts[0] + firsts[1]) + (firsts[2] + firsts[3])
    out[1] = (lasts[0] + lasts[1]) + (lasts[2] + lasts[3])


def block_solve(load, store, link, back, green_last):
    values = [load(0)]
    for i in range(1, B):
        values.append(load(i) + link[i] * values[-1])
    solved = values[-1] * green_last[B - 1]
    store(B - 1, solved)
    for i in range(B - 1, 0, -1):
        solved = back[i] * values[i - 1] + link[i] * solved
        store(i - 1, solved)


def chain_factors(count, coeffs, link, inv, carry):
    previous = None
    for i in range(1, count):
        pivot = coeffs[i - 1, 1] + coeffs[i, 0]
        if previous is not None:
            link[i] = coeffs[i - 1, 2] * previous
            pivot = pivot - coeffs[i - 1, 2] * link[i]
        previous = inverse(pivot)
        inv[i] = previous
        carry[i] = coeffs[i, 2] * previous


def chain_solve(count, ends, link, inv, carry, out):
    values = [None, ends[1, 0] - ends[0, 1]]
    for i in range(2, count):
        values.append((ends[i, 0] - ends[i - 1, 1]) + link[i] * values[-1])
    flux = values[count - 1] * inv[count - 1]
    out[count - 1] = flux
    for i in range(count - 2, 0, -1):
        flux = values[i] * inv[i] + carry[i] * flux
        out[i] = flux


def group_coefficients(coeffs, link, inv, carry, from_left, from_right, out):
    n = GROUP
    zero = jnp.zeros((B, NZ), jnp.float32)
    one = jnp.ones((B, NZ), jnp.float32)
    flux = carry[n - 1]
    from_right[n] = one
    from_right[0] = zero
    from_right[n - 1] = flux
    out[1] = coeffs[n - 1, 1] - coeffs[n - 1, 2] * flux
    for i in range(n - 2, 0, -1):
        flux = carry[i] * flux
        from_right[i] = flux
    out[2] = coeffs[0, 2] * flux
    values = [None, coeffs[0, 2]]
    for i in range(2, n):
        values.append(link[i] * values[-1])
    flux = values[n - 1] * inv[n - 1]
    from_left[0] = one
    from_left[n] = zero
    from_left[n - 1] = flux
    for i in range(n - 2, 0, -1):
        flux = values[i] * inv[i] + carry[i] * flux
        from_left[i] = flux
    out[0] = coeffs[0, 0] - coeffs[0, 2] * flux


def up(value, stride):
    return pltpu.roll(value, stride, axis=1)


def down(value, stride):
    return pltpu.roll(value, NZ - stride, axis=1)


def upright_bands(conduct):
    lane = lax.broadcasted_iota(jnp.int32, conduct.shape, 1)
    below = up(conduct, 1)
    face = (2.0 * conduct * below) * inverse(conduct + below)
    inner = jnp.where(lane == 0, 0.0, UPRIGHT * face)
    wall = jnp.where((lane == 0) | (lane == NZ - 1), UPRIGHT * conduct, 0.0)
    main = 1.0 + inner + down(inner, 1) + wall
    return inner, main


def upright_step(link, main, stride):
    inv = inverse(main)
    low = link * up(inv, stride)
    high = link * inv
    new_main = main - low * link - down(high * link, stride)
    return low, high, low * up(link, stride), new_main


def kernel(
    warmth_hbm,
    factor_hbm,
    out_ref,
    warmth,
    factor,
    half_x,
    warmth_t,
    conduct_t,
    half_y,
    side_t,
    side_n,
    halo,
    weights,
    scale_f,
    link_x,
    back_x,
    gf_x,
    gl_x,
    link_y,
    back_y,
    gf_y,
    gl_y,
    solved,
    co_z,
    co_x,
    co_r,
    end_z,
    end_x,
    end_r,
    ch_link,
    ch_inv,
    ch_carry,
    flux_z,
    flux_x,
    flux_r,
    from_left,
    from_right,
    load_sem,
    send_sem,
    recv_sem,
):
    row = lax.axis_index("row")
    col = lax.axis_index("col")
    me_x = col // GROUP
    me_z = lax.rem(col, GROUP)
    base = me_x * GROUP

    far_first = (4, 3, 5, 2, 6, 1, 7)
    z_peers = [(row, base + lax.rem(me_z + k, GROUP)) for k in far_first]
    x_peers = [(row, lax.rem(col + GROUP * k, GROUP * GROUPS)) for k in (2, 1, 3)]
    row_peers = [(lax.rem(row + k, ROWS), col) for k in far_first]
    columns = GROUP * GROUPS
    row_up, row_down = (lax.rem(row + 1, ROWS), col), (lax.rem(row + ROWS - 1, ROWS), col)
    col_up, col_down = (row, lax.rem(col + 1, columns)), (row, lax.rem(col + columns - 1, columns))

    barrier = pltpu.get_barrier_semaphore()
    everyone = [col_up, col_down] + row_peers + z_peers + x_peers
    for peer in everyone:
        pl.semaphore_signal(barrier, inc=1, device_id=peer, device_id_type=MESH)
    load_w = pltpu.make_async_copy(warmth_hbm, warmth, load_sem.at[0])
    load_f = pltpu.make_async_copy(factor_hbm, factor, load_sem.at[1])
    load_w.start()
    load_f.start()
    pl.semaphore_wait(barrier, len(everyone))

    def remote(src, dst, which, peer):
        return pltpu.make_async_remote_copy(
            src_ref=src,
            dst_ref=dst,
            send_sem=send_sem.at[which],
            recv_sem=recv_sem.at[which],
            device_id=peer,
            device_id_type=MESH,
        )

    for k, array in enumerate((warmth_hbm, factor_hbm)):
        remote(array.at[:, B - 1, :], halo.at[4 + k], 0, col_up).start()
        remote(array.at[:, 0, :], halo.at[6 + k], 0, col_down).start()
        remote(array.at[B - 1], halo.at[k], 0, row_up).start()
        remote(array.at[0], halo.at[2 + k], 0, row_down).start()

    def settle(buffer, count, sem):
        view = buffer.at[pl.ds(0, count)]
        pltpu.make_async_copy(view, view, sem).wait()

    def spread(buffer, index, which, peers):
        for peer in peers:
            remote(buffer.at[index], buffer.at[index], which, peer).start()

    load_w.wait()
    load_f.wait()

    before = None
    for i in range(B):
        w = warmth[i]
        c = conductivity(w, factor[i])
        h = half_resistance(c)
        half_x[i] = h
        warmth_t[pl.ds(i, B, stride=B), :] = w
        conduct_t[pl.ds(i, B, stride=B), :] = c
        half_y[pl.ds(i, B, stride=B), :] = h
        if before is None:
            edge_low_c = c
            flux_low = None
        else:
            flux_high = inverse(before[1] + h) * (w - before[0])
            gain = flux_high if flux_low is None else flux_high - flux_low
            side_t[pl.ds(i - 1, B, stride=B), :] = gain
            flux_low = flux_high
        before = (w, h)
    side_t[pl.ds(B - 1, B, stride=B), :] = -flux_low
    edge_high_c = c

    class Rows:
        def __init__(self, ref):
            self.ref = ref

        def __getitem__(self, i):
            return self.ref[i * B : (i + 1) * B, :]

    half_rows = Rows(half_y)
    block_coefficients(half_rows, link_y, back_y, gf_y, gl_y, co_z.at[me_z])
    spread(co_z, me_z, 1, z_peers)

    flux_low = None
    for i in range(B):
        if i < B - 1:
            flux_high = inverse(half_rows[i] + half_rows[i + 1]) * (
                warmth_t[(i + 1) * B : (i + 2) * B, :] - warmth_t[i * B : (i + 1) * B, :]
            )
        gain = flux_high if i == 0 else (-flux_low if i == B - 1 else flux_high - flux_low)
        side_t[i * B : (i + 1) * B, :] = side_t[i * B : (i + 1) * B, :] + gain
        flux_low = flux_high

    cells, last = B * B, B * (B - 1)
    lane = lax.broadcasted_iota(jnp.int32, (cells, NZ), 1)
    w = warmth_t[...]
    c = conduct_t[...]
    link, main = upright_bands(jnp.concatenate([c, edge_low_c, edge_high_c], axis=0))
    flux = jnp.where(lane == 0, UPRIGHT * c * (w - WARM_WALL), link[0:cells] * (w - up(w, 1)))
    flux_above = jnp.where(lane == NZ - 1, UPRIGHT * c * (CHILL_WALL - w), down(flux, 1))
    side = 2.0 * (side_t[...] + (flux_above - flux))

    def faces(value):
        return jnp.concatenate(
            [value[cells : cells + 2 * B], value[0:B], value[last : last + B]], axis=0
        )

    lows, highs = [], []
    for stride in STEPS:
        low, high, link, main = upright_step(link, main, stride)
        side = side + low[0:cells] * up(side, stride) + down(high[0:cells] * side, stride)
        lows.append(faces(low))
        highs.append(down(faces(high), stride))
    inv = inverse(main)
    side_t[...] = side * inv[0:cells]
    scale_f[...] = faces(inv)
    for n in range(0, len(STEPS) - 1, 2):
        wide = STEPS[n + 1]
        weights[3 * n] = lows[n] + lows[n + 1] * up(highs[n], wide)
        weights[3 * n + 1] = highs[n] + highs[n + 1] * down(lows[n], wide)
        weights[3 * n + 2] = lows[n + 1]
        weights[3 * n + 3] = highs[n + 1]
        weights[3 * n + 4] = lows[n + 1] * up(lows[n], wide)
        weights[3 * n + 5] = highs[n + 1] * down(highs[n], wide)
    weights[WEIGHTS - 1] = lows[-1] + highs[-1]

    settle(halo, 8, recv_sem.at[0])

    def through(near_w, near_h, k, present):
        other = halo[k]
        resist = near_h + half_resistance(conductivity(other, halo[k + 1]))
        return (2.0 * present) * (inverse(resist) * (other - near_w))

    def flag(condition):
        return jnp.where(condition, 1.0, 0.0).astype(jnp.float32)

    share = jnp.concatenate(
        [
            through(warmth[0], half_x[0], 0, flag(row > 0)),
            through(warmth[B - 1], half_x[B - 1], 2, flag(row < ROWS - 1)),
            through(warmth_t[0:B, :], half_rows[0], 4, flag(col > 0)),
            through(warmth_t[last : last + B, :], half_rows[B - 1], 6, flag(col < columns - 1)),
        ],
        axis=0,
    )
    for n in range(0, len(STEPS) - 1, 2):
        stride = STEPS[n]
        share = (
            (share + weights[3 * n] * up(share, stride))
            + (weights[3 * n + 1] * down(share, stride) + weights[3 * n + 2] * up(share, 2 * stride))
            + (weights[3 * n + 3] * down(share, 2 * stride) + weights[3 * n + 4] * up(share, 3 * stride))
            + weights[3 * n + 5] * down(share, 3 * stride)
        )
    share = (share + weights[WEIGHTS - 1] * up(share, STEPS[-1])) * scale_f[...]
    side_t[0:B, :] = side_t[0:B, :] + share[2 * B : 3 * B]
    side_t[last : last + B, :] = side_t[last : last + B, :] + share[3 * B : 4 * B]
    side_t[pl.ds(0, B, stride=B), :] = side_t[pl.ds(0, B, stride=B), :] + share[0:B]
    side_t[pl.ds(B - 1, B, stride=B), :] = side_t[pl.ds(B - 1, B, stride=B), :] + share[B : 2 * B]

    side_rows = Rows(side_t)
    block_ends(lambda i: side_rows[i], gf_y, gl_y, end_z.at[me_z])
    spread(end_z, me_z, 2, z_peers)

    settle(co_z, GROUP - 1, recv_sem.at[1])
    chain_factors(GROUP, co_z, ch_link.at[0], ch_inv.at[0], ch_carry.at[0])
    group_coefficients(
        co_z, ch_link.at[0], ch_inv.at[0], ch_carry.at[0], from_left, from_right, co_x.at[me_x]
    )
    spread(co_x, me_x, 3, x_peers)
    block_coefficients(half_x, link_x, back_x, gf_x, gl_x, co_r.at[row])
    spread(co_r, row, 4, row_peers)

    def keep(i, value):
        solved[i] = value

    block_solve(lambda i: side_rows[i], keep, link_y, back_y, gl_y)
    zero = jnp.zeros((B, NZ), jnp.float32)
    for ref, count in ((flux_z, GROUP), (flux_x, GROUPS), (flux_r, ROWS)):
        ref[0] = zero
        ref[count] = zero

    settle(end_z, GROUP - 1, recv_sem.at[2])
    chain_solve(GROUP, end_z, ch_link.at[0], ch_inv.at[0], ch_carry.at[0], flux_z)
    end_x[me_x, 0] = end_z[0, 0] + co_z[0, 2] * flux_z[1]
    end_x[me_x, 1] = end_z[GROUP - 1, 1] - co_z[GROUP - 1, 2] * flux_z[GROUP - 1]
    spread(end_x, me_x, 5, x_peers)

    settle(co_x, GROUPS - 1, recv_sem.at[3])
    chain_factors(GROUPS, co_x, ch_link.at[1], ch_inv.at[1], ch_carry.at[1])
    settle(co_r, ROWS - 1, recv_sem.at[4])
    chain_factors(ROWS, co_r, ch_link.at[2], ch_inv.at[2], ch_carry.at[2])

    settle(end_x, GROUPS - 1, recv_sem.at[5])
    chain_solve(GROUPS, end_x, ch_link.at[1], ch_inv.at[1], ch_carry.at[1], flux_x)
    outer_low, outer_high = flux_x[me_x], flux_x[me_x + 1]

    def inner_flux(i):
        return flux_z[i] + from_left[i] * outer_low + from_right[i] * outer_high

    flux_low, flux_high = inner_flux(me_z), inner_flux(me_z + 1)
    for i in range(B):
        side_n[pl.ds(i, B, stride=B), :] = solved[i] - gf_y[i] * flux_low + gl_y[i] * flux_high

    section = Rows(side_n)
    block_ends(lambda i: section[i], gf_x, gl_x, end_r.at[row])
    spread(end_r, row, 6, row_peers)
    block_solve(lambda i: section[i], keep, link_x, back_x, gl_x)

    settle(end_r, ROWS - 1, recv_sem.at[6])
    chain_solve(ROWS, end_r, ch_link.at[2], ch_inv.at[2], ch_carry.at[2], flux_r)
    flux_low, flux_high = flux_r[row], flux_r[row + 1]
    for i in range(B):
        out_ref[i] = warmth[i] + (solved[i] - gf_x[i] * flux_low + gl_x[i] * flux_high)

    settle(halo, 8, send_sem.at[0])
    settle(co_z, GROUP - 1, send_sem.at[1])
    settle(end_z, GROUP - 1, send_sem.at[2])
    settle(co_x, GROUPS - 1, send_sem.at[3])
    settle(co_r, ROWS - 1, send_sem.at[4])
    settle(end_x, GROUPS - 1, send_sem.at[5])
    settle(end_r, ROWS - 1, send_sem.at[6])


def shards(warmth, factor):
    def vmem(*shape):
        return pltpu.VMEM(shape, jnp.float32)

    scratch = [
        vmem(B, B, NZ),
        vmem(B, B, NZ),
        vmem(B, B, NZ),
        vmem(B * B, NZ),
        vmem(B * B, NZ),
        vmem(B * B, NZ),
        vmem(B * B, NZ),
        vmem(B * B, NZ),
        vmem(8, B, NZ),
        vmem(WEIGHTS, 4 * B, NZ),
        vmem(4 * B, NZ),
    ]
    scratch += [vmem(B, B, NZ) for _ in range(8)]
    scratch += [
        vmem(B, B, NZ),
        vmem(GROUP, 3, B, NZ),
        vmem(GROUPS, 3, B, NZ),
        vmem(ROWS, 3, B, NZ),
        vmem(GROUP, 2, B, NZ),
        vmem(GROUPS, 2, B, NZ),
        vmem(ROWS, 2, B, NZ),
        vmem(3, GROUP, B, NZ),
        vmem(3, GROUP, B, NZ),
        vmem(3, GROUP, B, NZ),
        vmem(GROUP + 1, B, NZ),
        vmem(GROUPS + 1, B, NZ),
        vmem(ROWS + 1, B, NZ),
        vmem(GROUP + 1, B, NZ),
        vmem(GROUP + 1, B, NZ),
        pltpu.SemaphoreType.DMA((2,)),
        pltpu.SemaphoreType.DMA((7,)),
        pltpu.SemaphoreType.DMA((7,)),
    ]
    return pl.pallas_call(
        kernel,
        out_shape=jax.ShapeDtypeStruct((B, B, NZ), jnp.float32),
        in_specs=[pl.BlockSpec(memory_space=pltpu.HBM)] * 2,
        out_specs=pl.BlockSpec(memory_space=pltpu.VMEM),
        scratch_shapes=scratch,
        compiler_params=pltpu.CompilerParams(
            collective_id=0, has_side_effects=True, vmem_limit_bytes=55040 * 1024
        ),
    )(warmth, factor)


def solution(mesh):
    return jax.shard_map(
        shards,
        mesh=mesh,
        in_specs=(P("row", "col", None), P("row", "col", None)),
        out_specs=P("row", "col", None),
        check_vma=False,
    )
```

```python
import functools

import jax
import jax.numpy as jnp
from jax import lax
from jax.experimental import pallas as pl
from jax.experimental.pallas import tpu as pltpu
from jax.sharding import PartitionSpec as P

MESH = pl.DeviceIdType.MESH
LATERAL = 1500.0
UPRIGHT = 2.0
WARM_WALL = 0.5
CHILL_WALL = -0.5
RESPONSE = 0.4
B = 16
NZ = 128
ROWS = 8
GROUP = 8
GROUPS = 4
STEPS = (1, 2, 4, 8, 16, 32, 64)
WEIGHTS = 19


def inverse(value):
    guess = pl.reciprocal(value, approx=True)
    return guess * (2.0 - value * guess)


def conductivity(temperature, factor):
    return factor * (1.0 + RESPONSE * jnp.tanh(temperature))


def half_resistance(conduct):
    return inverse((2.0 * LATERAL) * conduct)


def block_coefficients(half, link, back, green_first, green_last, out):
    left = jnp.ones((B, NZ), jnp.float32)
    right = jnp.ones((B, NZ), jnp.float32)
    lefts, rights = {}, {}
    for step in range(1, B):
        i, j = step, B - step
        resist = half[i - 1] + half[i]
        lefts[i] = inverse(1.0 + left * resist)
        link[i] = lefts[i]
        back[i] = lefts[i] * resist
        left = 1.0 + left * lefts[i]
        resist = half[j - 1] + half[j]
        rights[j] = inverse(1.0 + right * resist)
        right = 1.0 + right * rights[j]
    first, last = inverse(right), inverse(left)
    out[0] = first + half[0]
    out[1] = last + half[B - 1]
    green_first[0] = first
    green_last[B - 1] = last
    for i in range(1, B):
        first = first * rights[i]
        green_first[i] = first
        last = last * lefts[B - i]
        green_last[B - 1 - i] = last
    out[2] = first


def block_ends(load, green_first, green_last, out):
    firsts = [None] * 4
    lasts = [None] * 4
    for i in range(B):
        value = load(i)
        a, b = green_first[i] * value, green_last[i] * value
        k = i % 4
        firsts[k] = a if firsts[k] is None else firsts[k] + a
        lasts[k] = b if lasts[k] is None else lasts[k] + b
    out[0] = (firsts[0] + firsts[1]) + (firsts[2] + firsts[3])
    out[1] = (lasts[0] + lasts[1]) + (lasts[2] + lasts[3])


def block_solve(load, store, link, back, green_last):
    values = [load(0)]
    for i in range(1, B):
        values.append(load(i) + link[i] * values[-1])
    solved = values[-1] * green_last[B - 1]
    store(B - 1, solved)
    for i in range(B - 1, 0, -1):
        solved = back[i] * values[i - 1] + link[i] * solved
        store(i - 1, solved)


def chain_factors(count, coeffs, link, inv, carry):
    previous = None
    for i in range(1, count):
        pivot = coeffs[i - 1, 1] + coeffs[i, 0]
        if previous is not None:
            link[i] = coeffs[i - 1, 2] * previous
            pivot = pivot - coeffs[i - 1, 2] * link[i]
        previous = inverse(pivot)
        inv[i] = previous
        carry[i] = coeffs[i, 2] * previous


def chain_solve(count, ends, link, inv, carry, out):
    values = [None, ends[1, 0] - ends[0, 1]]
    for i in range(2, count):
        values.append((ends[i, 0] - ends[i - 1, 1]) + link[i] * values[-1])
    flux = values[count - 1] * inv[count - 1]
    out[count - 1] = flux
    for i in range(count - 2, 0, -1):
        flux = values[i] * inv[i] + carry[i] * flux
        out[i] = flux


def two_sided_factors(count, coeffs, left_inv, right_inv, left_link, right_link):
    zero = jnp.zeros((B, NZ), jnp.float32)
    left_inv[0] = zero
    right_inv[count] = zero
    below, above = zero, zero
    for i in range(1, count):
        j = count - i
        left_link[i - 1] = below
        pivot = coeffs[i - 1, 1] + coeffs[i, 0] - coeffs[i - 1, 2] * below
        pivot = inverse(pivot)
        left_inv[i] = pivot
        below = coeffs[i, 2] * pivot
        right_link[j] = above
        pivot = coeffs[j - 1, 1] + coeffs[j, 0] - coeffs[j, 2] * above
        pivot = inverse(pivot)
        right_inv[j] = pivot
        above = coeffs[j - 1, 2] * pivot
    left_link[count - 1] = below
    right_link[0] = above


def sweep_sides(count, parts, left_link, right_link, from_low, from_high):
    zero = jnp.zeros((B, NZ), jnp.float32)
    from_low[0] = zero
    from_high[count] = zero
    low, high = parts[0], parts[count - 1]
    from_low[1] = low
    from_high[count - 1] = high
    for i in range(1, count - 1):
        low = parts[i] + left_link[i] * low
        from_low[i + 1] = low
        high = parts[count - 1 - i] + right_link[count - 1 - i] * high
        from_high[count - 1 - i] = high


def group_coefficients(coeffs, link, inv, carry, from_left, from_right, out):
    n = GROUP
    zero = jnp.zeros((B, NZ), jnp.float32)
    one = jnp.ones((B, NZ), jnp.float32)
    flux = carry[n - 1]
    from_right[n] = one
    from_right[0] = zero
    from_right[n - 1] = flux
    out[1] = coeffs[n - 1, 1] - coeffs[n - 1, 2] * flux
    for i in range(n - 2, 0, -1):
        flux = carry[i] * flux
        from_right[i] = flux
    out[2] = coeffs[0, 2] * flux
    values = [None, coeffs[0, 2]]
    for i in range(2, n):
        values.append(link[i] * values[-1])
    flux = values[n - 1] * inv[n - 1]
    from_left[0] = one
    from_left[n] = zero
    from_left[n - 1] = flux
    for i in range(n - 2, 0, -1):
        flux = values[i] * inv[i] + carry[i] * flux
        from_left[i] = flux
    out[0] = coeffs[0, 0] - coeffs[0, 2] * flux


def up(value, stride):
    return pltpu.roll(value, stride, axis=1)


def down(value, stride):
    return pltpu.roll(value, NZ - stride, axis=1)


def upright_bands(conduct):
    lane = lax.broadcasted_iota(jnp.int32, conduct.shape, 1)
    below = up(conduct, 1)
    face = (2.0 * conduct * below) * inverse(conduct + below)
    inner = jnp.where(lane == 0, 0.0, UPRIGHT * face)
    wall = jnp.where((lane == 0) | (lane == NZ - 1), UPRIGHT * conduct, 0.0)
    main = 1.0 + inner + down(inner, 1) + wall
    return inner, main


def upright_step(link, main, stride):
    inv = inverse(main)
    low = link * up(inv, stride)
    high = link * inv
    new_main = main - low * link - down(high * link, stride)
    return low, high, low * up(link, stride), new_main


def kernel(
    warmth_hbm,
    factor_hbm,
    out_ref,
    warmth,
    factor,
    half_x,
    warmth_t,
    conduct_t,
    half_y,
    side_t,
    side_n,
    halo,
    edges,
    weights,
    scale_f,
    link_x,
    back_x,
    gf_x,
    gl_x,
    link_y,
    back_y,
    gf_y,
    gl_y,
    solved,
    co_z,
    co_x,
    co_r,
    end_z,
    end_x,
    end_r,
    ch_link,
    ch_inv,
    ch_carry,
    flux_z,
    flux_x,
    ends,
    parts,
    left_inv,
    right_inv,
    left_link,
    right_link,
    from_low,
    from_high,
    from_left,
    from_right,
    load_sem,
    send_sem,
    recv_sem,
):
    row = lax.axis_index("row")
    col = lax.axis_index("col")
    me_x = col // GROUP
    me_z = lax.rem(col, GROUP)
    base = me_x * GROUP

    far_first = (4, 3, 5, 2, 6, 1, 7)
    z_peers = [(row, base + lax.rem(me_z + k, GROUP)) for k in far_first]
    x_peers = [(row, lax.rem(col + GROUP * k, GROUP * GROUPS)) for k in (2, 1, 3)]
    row_peers = [(lax.rem(row + k, ROWS), col) for k in far_first]
    columns = GROUP * GROUPS
    row_up, row_down = (lax.rem(row + 1, ROWS), col), (lax.rem(row + ROWS - 1, ROWS), col)
    col_up, col_down = (row, lax.rem(col + 1, columns)), (row, lax.rem(col + columns - 1, columns))

    barrier = pltpu.get_barrier_semaphore()
    everyone = [col_up, col_down] + row_peers + z_peers + x_peers
    for peer in everyone:
        pl.semaphore_signal(barrier, inc=1, device_id=peer, device_id_type=MESH)
    load_w = pltpu.make_async_copy(warmth_hbm, warmth, load_sem.at[0])
    load_f = pltpu.make_async_copy(factor_hbm, factor, load_sem.at[1])
    load_w.start()
    load_f.start()
    load_w.wait()
    load_f.wait()
    for k, array in enumerate((warmth, factor)):
        edges[0, k] = array[B - 1]
        edges[1, k] = array[0]
        edges[2, k] = array[:, B - 1, :]
        edges[3, k] = array[:, 0, :]

    def remote(src, dst, which, peer):
        return pltpu.make_async_remote_copy(
            src_ref=src,
            dst_ref=dst,
            send_sem=send_sem.at[which],
            recv_sem=recv_sem.at[which],
            device_id=peer,
            device_id_type=MESH,
        )

    pl.semaphore_wait(barrier, len(everyone))
    for k, peer in enumerate((row_up, row_down, col_up, col_down)):
        remote(edges.at[k], halo.at[k], 0, peer).start()

    def settle(buffer, count, sem):
        view = buffer.at[pl.ds(0, count)]
        pltpu.make_async_copy(view, view, sem).wait()

    def spread(buffer, index, which, peers):
        for peer in peers:
            remote(buffer.at[index], buffer.at[index], which, peer).start()


    before = None
    for i in range(B):
        w = warmth[i]
        c = conductivity(w, factor[i])
        h = half_resistance(c)
        half_x[i] = h
        warmth_t[pl.ds(i, B, stride=B), :] = w
        conduct_t[pl.ds(i, B, stride=B), :] = c
        half_y[pl.ds(i, B, stride=B), :] = h
        if before is None:
            edge_low_c = c
            flux_low = None
        else:
            flux_high = inverse(before[1] + h) * (w - before[0])
            gain = flux_high if flux_low is None else flux_high - flux_low
            side_t[pl.ds(i - 1, B, stride=B), :] = gain
            flux_low = flux_high
        before = (w, h)
    side_t[pl.ds(B - 1, B, stride=B), :] = -flux_low
    edge_high_c = c

    class Rows:
        def __init__(self, ref):
            self.ref = ref

        def __getitem__(self, i):
            return self.ref[i * B : (i + 1) * B, :]

    half_rows = Rows(half_y)
    block_coefficients(half_rows, link_y, back_y, gf_y, gl_y, co_z.at[me_z])
    spread(co_z, me_z, 1, z_peers)

    flux_low = None
    for i in range(B):
        if i < B - 1:
            flux_high = inverse(half_rows[i] + half_rows[i + 1]) * (
                warmth_t[(i + 1) * B : (i + 2) * B, :] - warmth_t[i * B : (i + 1) * B, :]
            )
        gain = flux_high if i == 0 else (-flux_low if i == B - 1 else flux_high - flux_low)
        side_t[i * B : (i + 1) * B, :] = side_t[i * B : (i + 1) * B, :] + gain
        flux_low = flux_high

    cells, last = B * B, B * (B - 1)
    lane = lax.broadcasted_iota(jnp.int32, (cells, NZ), 1)
    w = warmth_t[...]
    c = conduct_t[...]
    link, main = upright_bands(jnp.concatenate([c, edge_low_c, edge_high_c], axis=0))
    flux = jnp.where(lane == 0, UPRIGHT * c * (w - WARM_WALL), link[0:cells] * (w - up(w, 1)))
    flux_above = jnp.where(lane == NZ - 1, UPRIGHT * c * (CHILL_WALL - w), down(flux, 1))
    side = 2.0 * (side_t[...] + (flux_above - flux))

    def faces(value):
        return jnp.concatenate(
            [value[cells : cells + 2 * B], value[0:B], value[last : last + B]], axis=0
        )

    lows, highs = [], []
    for stride in STEPS:
        low, high, link, main = upright_step(link, main, stride)
        side = side + low[0:cells] * up(side, stride) + down(high[0:cells] * side, stride)
        lows.append(faces(low))
        highs.append(down(faces(high), stride))
    inv = inverse(main)
    side_t[...] = side * inv[0:cells]
    scale_f[...] = faces(inv)
    for n in range(0, len(STEPS) - 1, 2):
        wide = STEPS[n + 1]
        weights[3 * n] = lows[n] + lows[n + 1] * up(highs[n], wide)
        weights[3 * n + 1] = highs[n] + highs[n + 1] * down(lows[n], wide)
        weights[3 * n + 2] = lows[n + 1]
        weights[3 * n + 3] = highs[n + 1]
        weights[3 * n + 4] = lows[n + 1] * up(lows[n], wide)
        weights[3 * n + 5] = highs[n + 1] * down(highs[n], wide)
    weights[WEIGHTS - 1] = lows[-1] + highs[-1]

    settle(halo, 4, recv_sem.at[0])

    def through(near_w, near_h, k, present):
        other = halo[k, 0]
        resist = near_h + half_resistance(conductivity(other, halo[k, 1]))
        return (2.0 * present) * (inverse(resist) * (other - near_w))

    def flag(condition):
        return jnp.where(condition, 1.0, 0.0).astype(jnp.float32)

    share = jnp.concatenate(
        [
            through(warmth[0], half_x[0], 0, flag(row > 0)),
            through(warmth[B - 1], half_x[B - 1], 1, flag(row < ROWS - 1)),
            through(warmth_t[0:B, :], half_rows[0], 2, flag(col > 0)),
            through(warmth_t[last : last + B, :], half_rows[B - 1], 3, flag(col < columns - 1)),
        ],
        axis=0,
    )
    for n in range(0, len(STEPS) - 1, 2):
        stride = STEPS[n]
        share = (
            (share + weights[3 * n] * up(share, stride))
            + (weights[3 * n + 1] * down(share, stride) + weights[3 * n + 2] * up(share, 2 * stride))
            + (weights[3 * n + 3] * down(share, 2 * stride) + weights[3 * n + 4] * up(share, 3 * stride))
            + weights[3 * n + 5] * down(share, 3 * stride)
        )
    share = (share + weights[WEIGHTS - 1] * up(share, STEPS[-1])) * scale_f[...]
    side_t[0:B, :] = side_t[0:B, :] + share[2 * B : 3 * B]
    side_t[last : last + B, :] = side_t[last : last + B, :] + share[3 * B : 4 * B]
    side_t[pl.ds(0, B, stride=B), :] = side_t[pl.ds(0, B, stride=B), :] + share[0:B]
    side_t[pl.ds(B - 1, B, stride=B), :] = side_t[pl.ds(B - 1, B, stride=B), :] + share[B : 2 * B]

    side_rows = Rows(side_t)
    block_ends(lambda i: side_rows[i], gf_y, gl_y, end_z.at[me_z])
    spread(end_z, me_z, 2, z_peers)

    settle(co_z, GROUP - 1, recv_sem.at[1])
    chain_factors(GROUP, co_z, ch_link.at[0], ch_inv.at[0], ch_carry.at[0])
    group_coefficients(
        co_z, ch_link.at[0], ch_inv.at[0], ch_carry.at[0], from_left, from_right, co_x.at[me_x]
    )
    spread(co_x, me_x, 3, x_peers)
    block_coefficients(half_x, link_x, back_x, gf_x, gl_x, co_r.at[row])
    spread(co_r, row, 4, row_peers)

    def keep(i, value):
        solved[i] = value

    block_solve(lambda i: side_rows[i], keep, link_y, back_y, gl_y)
    zero = jnp.zeros((B, NZ), jnp.float32)
    for ref, count in ((flux_z, GROUP), (flux_x, GROUPS)):
        ref[0] = zero
        ref[count] = zero

    settle(end_z, GROUP - 1, recv_sem.at[2])
    chain_solve(GROUP, end_z, ch_link.at[0], ch_inv.at[0], ch_carry.at[0], flux_z)
    end_x[me_x, 0] = end_z[0, 0] + co_z[0, 2] * flux_z[1]
    end_x[me_x, 1] = end_z[GROUP - 1, 1] - co_z[GROUP - 1, 2] * flux_z[GROUP - 1]
    spread(end_x, me_x, 5, x_peers)

    settle(co_x, GROUPS - 1, recv_sem.at[3])
    chain_factors(GROUPS, co_x, ch_link.at[1], ch_inv.at[1], ch_carry.at[1])
    settle(co_r, ROWS - 1, recv_sem.at[4])
    two_sided_factors(ROWS, co_r, left_inv, right_inv, left_link, right_link)
    own_left, own_right, own_link = left_inv[row], right_inv[row + 1], co_r[row, 2]
    to_high = own_link * own_left
    to_low = own_link * own_right
    weight_high = own_right * inverse(1.0 - to_high * to_low)
    weight_cross = to_high * weight_high
    weight_low = own_left * (1.0 + own_link * weight_cross)

    settle(end_x, GROUPS - 1, recv_sem.at[5])
    chain_solve(GROUPS, end_x, ch_link.at[1], ch_inv.at[1], ch_carry.at[1], flux_x)
    outer_low, outer_high = flux_x[me_x], flux_x[me_x + 1]

    def inner_flux(i):
        return flux_z[i] + from_left[i] * outer_low + from_right[i] * outer_high

    flux_low, flux_high = inner_flux(me_z), inner_flux(me_z + 1)
    for i in range(B):
        side_n[pl.ds(i, B, stride=B), :] = solved[i] - gf_y[i] * flux_low + gl_y[i] * flux_high

    section = Rows(side_n)
    block_ends(lambda i: section[i], gf_x, gl_x, ends)
    own_first, own_last = ends[0], ends[1]
    parts[0] = to_high * own_first - own_last
    parts[1] = own_first - to_low * own_last
    end_r[row] = own_first
    for peer in row_peers:
        side = jnp.where(peer[0] > row, 0, 1)
        remote(parts.at[side], end_r.at[row], 6, peer).start()
    block_solve(lambda i: section[i], keep, link_x, back_x, gl_x)

    settle(end_r, ROWS - 1, recv_sem.at[6])
    sweep_sides(ROWS, end_r, left_link, right_link, from_low, from_high)
    low_side = own_first + from_low[row]
    high_side = from_high[row + 1] - own_last
    flux_low = weight_low * low_side + weight_cross * high_side
    flux_high = weight_cross * low_side + weight_high * high_side
    for i in range(B):
        out_ref[i] = warmth[i] + (solved[i] - gf_x[i] * flux_low + gl_x[i] * flux_high)

    settle(halo, 4, send_sem.at[0])
    settle(co_z, GROUP - 1, send_sem.at[1])
    settle(end_z, GROUP - 1, send_sem.at[2])
    settle(co_x, GROUPS - 1, send_sem.at[3])
    settle(co_r, ROWS - 1, send_sem.at[4])
    settle(end_x, GROUPS - 1, send_sem.at[5])
    settle(end_r, ROWS - 1, send_sem.at[6])


def shards(warmth, factor):
    def vmem(*shape):
        return pltpu.VMEM(shape, jnp.float32)

    scratch = [
        vmem(B, B, NZ),
        vmem(B, B, NZ),
        vmem(B, B, NZ),
        vmem(B * B, NZ),
        vmem(B * B, NZ),
        vmem(B * B, NZ),
        vmem(B * B, NZ),
        vmem(B * B, NZ),
        vmem(4, 2, B, NZ),
        vmem(4, 2, B, NZ),
        vmem(WEIGHTS, 4 * B, NZ),
        vmem(4 * B, NZ),
    ]
    scratch += [vmem(B, B, NZ) for _ in range(8)]
    scratch += [
        vmem(B, B, NZ),
        vmem(GROUP, 3, B, NZ),
        vmem(GROUPS, 3, B, NZ),
        vmem(ROWS, 3, B, NZ),
        vmem(GROUP, 2, B, NZ),
        vmem(GROUPS, 2, B, NZ),
        vmem(ROWS, B, NZ),
        vmem(2, GROUP, B, NZ),
        vmem(2, GROUP, B, NZ),
        vmem(2, GROUP, B, NZ),
        vmem(GROUP + 1, B, NZ),
        vmem(GROUPS + 1, B, NZ),
        vmem(2, B, NZ),
        vmem(2, B, NZ),
        vmem(ROWS + 1, B, NZ),
        vmem(ROWS + 1, B, NZ),
        vmem(ROWS, B, NZ),
        vmem(ROWS, B, NZ),
        vmem(ROWS + 1, B, NZ),
        vmem(ROWS + 1, B, NZ),
        vmem(GROUP + 1, B, NZ),
        vmem(GROUP + 1, B, NZ),
        pltpu.SemaphoreType.DMA((2,)),
        pltpu.SemaphoreType.DMA((7,)),
        pltpu.SemaphoreType.DMA((7,)),
    ]
    return pl.pallas_call(
        kernel,
        out_shape=jax.ShapeDtypeStruct((B, B, NZ), jnp.float32),
        in_specs=[pl.BlockSpec(memory_space=pltpu.HBM)] * 2,
        out_specs=pl.BlockSpec(memory_space=pltpu.VMEM),
        scratch_shapes=scratch,
        compiler_params=pltpu.CompilerParams(
            collective_id=0, has_side_effects=True, vmem_limit_bytes=55040 * 1024
        ),
    )(warmth, factor)


def solution(mesh):
    return jax.shard_map(
        shards,
        mesh=mesh,
        in_specs=(P("row", "col", None), P("row", "col", None)),
        out_specs=P("row", "col", None),
        check_vma=False,
    )
```

```python
import functools

import jax
import jax.numpy as jnp
from jax import lax
from jax.experimental import pallas as pl
from jax.experimental.pallas import tpu as pltpu
from jax.sharding import PartitionSpec as P

MESH = pl.DeviceIdType.MESH
LATERAL = 1500.0
UPRIGHT = 2.0
WARM_WALL = 0.5
CHILL_WALL = -0.5
RESPONSE = 0.4
B = 16
NZ = 128
ROWS = 8
GROUP = 8
GROUPS = 4
STEPS = (1, 2, 4, 8, 16, 32, 64)
WEIGHTS = 19


def inverse(value):
    guess = pl.reciprocal(value, approx=True)
    return guess * (2.0 - value * guess)


def conductivity(temperature, factor):
    return factor * (1.0 + RESPONSE * jnp.tanh(temperature))


def half_resistance(conduct):
    return inverse((2.0 * LATERAL) * conduct)


def block_coefficients(half, link, back, green_first, green_last, out):
    left = jnp.ones((B, NZ), jnp.float32)
    right = jnp.ones((B, NZ), jnp.float32)
    lefts, rights = {}, {}
    for step in range(1, B):
        i, j = step, B - step
        resist = half[i - 1] + half[i]
        lefts[i] = inverse(1.0 + left * resist)
        link[i] = lefts[i]
        back[i] = lefts[i] * resist
        left = 1.0 + left * lefts[i]
        resist = half[j - 1] + half[j]
        rights[j] = inverse(1.0 + right * resist)
        right = 1.0 + right * rights[j]
    first, last = inverse(right), inverse(left)
    out[0] = first + half[0]
    out[1] = last + half[B - 1]
    green_first[0] = first
    green_last[B - 1] = last
    for i in range(1, B):
        first = first * rights[i]
        green_first[i] = first
        last = last * lefts[B - i]
        green_last[B - 1 - i] = last
    out[2] = first


def block_ends(load, green_first, green_last, out):
    firsts = [None] * 4
    lasts = [None] * 4
    for i in range(B):
        value = load(i)
        a, b = green_first[i] * value, green_last[i] * value
        k = i % 4
        firsts[k] = a if firsts[k] is None else firsts[k] + a
        lasts[k] = b if lasts[k] is None else lasts[k] + b
    out[0] = (firsts[0] + firsts[1]) + (firsts[2] + firsts[3])
    out[1] = (lasts[0] + lasts[1]) + (lasts[2] + lasts[3])


def block_solve(load, store, link, back, green_last):
    values = [load(0)]
    for i in range(1, B):
        values.append(load(i) + link[i] * values[-1])
    solved = values[-1] * green_last[B - 1]
    store(B - 1, solved)
    for i in range(B - 1, 0, -1):
        solved = back[i] * values[i - 1] + link[i] * solved
        store(i - 1, solved)


def chain_factors(count, coeffs, link, inv, carry):
    previous = None
    for i in range(1, count):
        pivot = coeffs[i - 1, 1] + coeffs[i, 0]
        if previous is not None:
            link[i] = coeffs[i - 1, 2] * previous
            pivot = pivot - coeffs[i - 1, 2] * link[i]
        previous = inverse(pivot)
        inv[i] = previous
        carry[i] = coeffs[i, 2] * previous


def chain_solve(count, ends, link, inv, carry, out):
    values = [None, ends[1, 0] - ends[0, 1]]
    for i in range(2, count):
        values.append((ends[i, 0] - ends[i - 1, 1]) + link[i] * values[-1])
    flux = values[count - 1] * inv[count - 1]
    out[count - 1] = flux
    for i in range(count - 2, 0, -1):
        flux = values[i] * inv[i] + carry[i] * flux
        out[i] = flux


def two_sided_factors(count, coeffs, left_inv, right_inv, left_link, right_link):
    zero = jnp.zeros((B, NZ), jnp.float32)
    left_inv[0] = zero
    right_inv[count] = zero
    below, above = zero, zero
    for i in range(1, count):
        j = count - i
        left_link[i - 1] = below
        pivot = coeffs[i - 1, 1] + coeffs[i, 0] - coeffs[i - 1, 2] * below
        pivot = inverse(pivot)
        left_inv[i] = pivot
        below = coeffs[i, 2] * pivot
        right_link[j] = above
        pivot = coeffs[j - 1, 1] + coeffs[j, 0] - coeffs[j, 2] * above
        pivot = inverse(pivot)
        right_inv[j] = pivot
        above = coeffs[j - 1, 2] * pivot
    left_link[count - 1] = below
    right_link[0] = above


def sweep_sides(count, parts, left_link, right_link, from_low, from_high):
    zero = jnp.zeros((B, NZ), jnp.float32)
    from_low[0] = zero
    from_high[count] = zero
    low, high = parts[0], parts[count - 1]
    from_low[1] = low
    from_high[count - 1] = high
    for i in range(1, count - 1):
        low = parts[i] + left_link[i] * low
        from_low[i + 1] = low
        high = parts[count - 1 - i] + right_link[count - 1 - i] * high
        from_high[count - 1 - i] = high


def group_coefficients(coeffs, link, inv, carry, from_left, from_right, out):
    n = GROUP
    zero = jnp.zeros((B, NZ), jnp.float32)
    one = jnp.ones((B, NZ), jnp.float32)
    flux = carry[n - 1]
    from_right[n] = one
    from_right[0] = zero
    from_right[n - 1] = flux
    out[1] = coeffs[n - 1, 1] - coeffs[n - 1, 2] * flux
    for i in range(n - 2, 0, -1):
        flux = carry[i] * flux
        from_right[i] = flux
    out[2] = coeffs[0, 2] * flux
    values = [None, coeffs[0, 2]]
    for i in range(2, n):
        values.append(link[i] * values[-1])
    flux = values[n - 1] * inv[n - 1]
    from_left[0] = one
    from_left[n] = zero
    from_left[n - 1] = flux
    for i in range(n - 2, 0, -1):
        flux = values[i] * inv[i] + carry[i] * flux
        from_left[i] = flux
    out[0] = coeffs[0, 0] - coeffs[0, 2] * flux


def up(value, stride):
    return pltpu.roll(value, stride, axis=1)


def down(value, stride):
    return pltpu.roll(value, NZ - stride, axis=1)


def upright_bands(conduct):
    lane = lax.broadcasted_iota(jnp.int32, conduct.shape, 1)
    below = up(conduct, 1)
    face = (2.0 * conduct * below) * inverse(conduct + below)
    inner = jnp.where(lane == 0, 0.0, UPRIGHT * face)
    wall = jnp.where((lane == 0) | (lane == NZ - 1), UPRIGHT * conduct, 0.0)
    main = 1.0 + inner + down(inner, 1) + wall
    return inner, main


def upright_step(link, main, stride):
    inv = inverse(main)
    low = link * up(inv, stride)
    high = link * inv
    new_main = main - low * link - down(high * link, stride)
    return low, high, low * up(link, stride), new_main


def kernel(
    warmth_hbm,
    factor_hbm,
    out_ref,
    warmth,
    factor,
    half_x,
    warmth_t,
    conduct_t,
    half_y,
    side_t,
    side_n,
    halo,
    edges,
    weights,
    scale_f,
    link_x,
    back_x,
    gf_x,
    gl_x,
    link_y,
    back_y,
    gf_y,
    gl_y,
    solved,
    co_z,
    co_x,
    co_r,
    end_z,
    end_x,
    end_r,
    ch_link,
    ch_inv,
    ch_carry,
    flux_z,
    flux_x,
    ends,
    parts,
    left_inv,
    right_inv,
    left_link,
    right_link,
    from_low,
    from_high,
    from_left,
    from_right,
    load_sem,
    send_sem,
    recv_sem,
):
    row = lax.axis_index("row")
    col = lax.axis_index("col")
    me_x = col // GROUP
    me_z = lax.rem(col, GROUP)
    base = me_x * GROUP

    far_first = (4, 3, 5, 2, 6, 1, 7)
    z_peers = [(row, base + lax.rem(me_z + k, GROUP)) for k in far_first]
    x_peers = [(row, lax.rem(col + GROUP * k, GROUP * GROUPS)) for k in (2, 1, 3)]
    row_peers = [(lax.rem(row + k, ROWS), col) for k in far_first]
    columns = GROUP * GROUPS
    row_up, row_down = (lax.rem(row + 1, ROWS), col), (lax.rem(row + ROWS - 1, ROWS), col)
    col_up, col_down = (row, lax.rem(col + 1, columns)), (row, lax.rem(col + columns - 1, columns))

    barrier = pltpu.get_barrier_semaphore()
    everyone = [col_up, col_down] + row_peers + z_peers + x_peers
    for peer in everyone:
        pl.semaphore_signal(barrier, inc=1, device_id=peer, device_id_type=MESH)
    load_w = pltpu.make_async_copy(warmth_hbm, warmth, load_sem.at[0])
    load_f = pltpu.make_async_copy(factor_hbm, factor, load_sem.at[1])
    load_w.start()
    load_f.start()
    load_w.wait()
    load_f.wait()
    for k, array in enumerate((warmth, factor)):
        edges[0, k] = array[B - 1]
        edges[1, k] = array[0]
        edges[2, k] = array[:, B - 1, :]
        edges[3, k] = array[:, 0, :]

    def remote(src, dst, which, peer):
        return pltpu.make_async_remote_copy(
            src_ref=src,
            dst_ref=dst,
            send_sem=send_sem.at[which],
            recv_sem=recv_sem.at[which],
            device_id=peer,
            device_id_type=MESH,
        )

    pl.semaphore_wait(barrier, len(everyone))
    for k, peer in ((2, col_up), (3, col_down), (0, row_up), (1, row_down)):
        remote(edges.at[k], halo.at[k], 0, peer).start()

    def settle(buffer, count, sem):
        view = buffer.at[pl.ds(0, count)]
        pltpu.make_async_copy(view, view, sem).wait()

    def spread(buffer, index, which, peers):
        for peer in peers:
            remote(buffer.at[index], buffer.at[index], which, peer).start()


    before = None
    for i in range(B):
        w = warmth[i]
        c = conductivity(w, factor[i])
        h = half_resistance(c)
        half_x[i] = h
        warmth_t[pl.ds(i, B, stride=B), :] = w
        conduct_t[pl.ds(i, B, stride=B), :] = c
        half_y[pl.ds(i, B, stride=B), :] = h
        if before is None:
            edge_low_c = c
            flux_low = None
        else:
            flux_high = inverse(before[1] + h) * (w - before[0])
            gain = flux_high if flux_low is None else flux_high - flux_low
            side_t[pl.ds(i - 1, B, stride=B), :] = gain
            flux_low = flux_high
        before = (w, h)
    side_t[pl.ds(B - 1, B, stride=B), :] = -flux_low
    edge_high_c = c

    class Rows:
        def __init__(self, ref):
            self.ref = ref

        def __getitem__(self, i):
            return self.ref[i * B : (i + 1) * B, :]

    half_rows = Rows(half_y)
    block_coefficients(half_rows, link_y, back_y, gf_y, gl_y, co_z.at[me_z])
    spread(co_z, me_z, 1, z_peers[::-1])

    flux_low = None
    for i in range(B):
        if i < B - 1:
            flux_high = inverse(half_rows[i] + half_rows[i + 1]) * (
                warmth_t[(i + 1) * B : (i + 2) * B, :] - warmth_t[i * B : (i + 1) * B, :]
            )
        gain = flux_high if i == 0 else (-flux_low if i == B - 1 else flux_high - flux_low)
        side_t[i * B : (i + 1) * B, :] = side_t[i * B : (i + 1) * B, :] + gain
        flux_low = flux_high

    cells, last = B * B, B * (B - 1)
    lane = lax.broadcasted_iota(jnp.int32, (cells, NZ), 1)
    w = warmth_t[...]
    c = conduct_t[...]
    link, main = upright_bands(jnp.concatenate([c, edge_low_c, edge_high_c], axis=0))
    flux = jnp.where(lane == 0, UPRIGHT * c * (w - WARM_WALL), link[0:cells] * (w - up(w, 1)))
    flux_above = jnp.where(lane == NZ - 1, UPRIGHT * c * (CHILL_WALL - w), down(flux, 1))
    side = 2.0 * (side_t[...] + (flux_above - flux))

    def faces(value):
        return jnp.concatenate(
            [value[cells : cells + 2 * B], value[0:B], value[last : last + B]], axis=0
        )

    lows, highs = [], []
    for stride in STEPS:
        low, high, link, main = upright_step(link, main, stride)
        side = side + low[0:cells] * up(side, stride) + down(high[0:cells] * side, stride)
        lows.append(faces(low))
        highs.append(down(faces(high), stride))
    inv = inverse(main)
    side_t[...] = side * inv[0:cells]
    scale_f[...] = faces(inv)
    for n in range(0, len(STEPS) - 1, 2):
        wide = STEPS[n + 1]
        weights[3 * n] = lows[n] + lows[n + 1] * up(highs[n], wide)
        weights[3 * n + 1] = highs[n] + highs[n + 1] * down(lows[n], wide)
        weights[3 * n + 2] = lows[n + 1]
        weights[3 * n + 3] = highs[n + 1]
        weights[3 * n + 4] = lows[n + 1] * up(lows[n], wide)
        weights[3 * n + 5] = highs[n + 1] * down(highs[n], wide)
    weights[WEIGHTS - 1] = lows[-1] + highs[-1]

    settle(halo, 4, recv_sem.at[0])

    def through(near_w, near_h, k, present):
        other = halo[k, 0]
        resist = near_h + half_resistance(conductivity(other, halo[k, 1]))
        return (2.0 * present) * (inverse(resist) * (other - near_w))

    def flag(condition):
        return jnp.where(condition, 1.0, 0.0).astype(jnp.float32)

    share = jnp.concatenate(
        [
            through(warmth[0], half_x[0], 0, flag(row > 0)),
            through(warmth[B - 1], half_x[B - 1], 1, flag(row < ROWS - 1)),
            through(warmth_t[0:B, :], half_rows[0], 2, flag(col > 0)),
            through(warmth_t[last : last + B, :], half_rows[B - 1], 3, flag(col < columns - 1)),
        ],
        axis=0,
    )
    for n in range(0, len(STEPS) - 1, 2):
        stride = STEPS[n]
        share = (
            (share + weights[3 * n] * up(share, stride))
            + (weights[3 * n + 1] * down(share, stride) + weights[3 * n + 2] * up(share, 2 * stride))
            + (weights[3 * n + 3] * down(share, 2 * stride) + weights[3 * n + 4] * up(share, 3 * stride))
            + weights[3 * n + 5] * down(share, 3 * stride)
        )
    share = (share + weights[WEIGHTS - 1] * up(share, STEPS[-1])) * scale_f[...]
    side_t[0:B, :] = side_t[0:B, :] + share[2 * B : 3 * B]
    side_t[last : last + B, :] = side_t[last : last + B, :] + share[3 * B : 4 * B]
    side_t[pl.ds(0, B, stride=B), :] = side_t[pl.ds(0, B, stride=B), :] + share[0:B]
    side_t[pl.ds(B - 1, B, stride=B), :] = side_t[pl.ds(B - 1, B, stride=B), :] + share[B : 2 * B]

    side_rows = Rows(side_t)
    block_ends(lambda i: side_rows[i], gf_y, gl_y, end_z.at[me_z])
    spread(end_z, me_z, 2, z_peers)

    settle(co_z, GROUP - 1, recv_sem.at[1])
    chain_factors(GROUP, co_z, ch_link.at[0], ch_inv.at[0], ch_carry.at[0])
    group_coefficients(
        co_z, ch_link.at[0], ch_inv.at[0], ch_carry.at[0], from_left, from_right, co_x.at[me_x]
    )
    spread(co_x, me_x, 3, x_peers)
    block_coefficients(half_x, link_x, back_x, gf_x, gl_x, co_r.at[row])
    spread(co_r, row, 4, row_peers)

    def keep(i, value):
        solved[i] = value

    block_solve(lambda i: side_rows[i], keep, link_y, back_y, gl_y)
    zero = jnp.zeros((B, NZ), jnp.float32)
    for ref, count in ((flux_z, GROUP), (flux_x, GROUPS)):
        ref[0] = zero
        ref[count] = zero

    settle(end_z, GROUP - 1, recv_sem.at[2])
    chain_solve(GROUP, end_z, ch_link.at[0], ch_inv.at[0], ch_carry.at[0], flux_z)
    end_x[me_x, 0] = end_z[0, 0] + co_z[0, 2] * flux_z[1]
    end_x[me_x, 1] = end_z[GROUP - 1, 1] - co_z[GROUP - 1, 2] * flux_z[GROUP - 1]
    spread(end_x, me_x, 5, x_peers)

    settle(co_x, GROUPS - 1, recv_sem.at[3])
    chain_factors(GROUPS, co_x, ch_link.at[1], ch_inv.at[1], ch_carry.at[1])
    settle(co_r, ROWS - 1, recv_sem.at[4])
    two_sided_factors(ROWS, co_r, left_inv, right_inv, left_link, right_link)
    own_left, own_right, own_link = left_inv[row], right_inv[row + 1], co_r[row, 2]
    to_high = own_link * own_left
    to_low = own_link * own_right
    weight_high = own_right * inverse(1.0 - to_high * to_low)
    weight_cross = to_high * weight_high
    weight_low = own_left * (1.0 + own_link * weight_cross)

    settle(end_x, GROUPS - 1, recv_sem.at[5])
    chain_solve(GROUPS, end_x, ch_link.at[1], ch_inv.at[1], ch_carry.at[1], flux_x)
    outer_low, outer_high = flux_x[me_x], flux_x[me_x + 1]

    def inner_flux(i):
        return flux_z[i] + from_left[i] * outer_low + from_right[i] * outer_high

    flux_low, flux_high = inner_flux(me_z), inner_flux(me_z + 1)
    for i in range(B):
        side_n[pl.ds(i, B, stride=B), :] = solved[i] - gf_y[i] * flux_low + gl_y[i] * flux_high

    section = Rows(side_n)
    block_ends(lambda i: section[i], gf_x, gl_x, ends)
    own_first, own_last = ends[0], ends[1]
    parts[0] = to_high * own_first - own_last
    parts[1] = own_first - to_low * own_last
    end_r[row] = own_first
    for peer in row_peers:
        side = jnp.where(peer[0] > row, 0, 1)
        remote(parts.at[side], end_r.at[row], 6, peer).start()
    block_solve(lambda i: section[i], keep, link_x, back_x, gl_x)

    settle(end_r, ROWS - 1, recv_sem.at[6])
    sweep_sides(ROWS, end_r, left_link, right_link, from_low, from_high)
    low_side = own_first + from_low[row]
    high_side = from_high[row + 1] - own_last
    flux_low = weight_low * low_side + weight_cross * high_side
    flux_high = weight_cross * low_side + weight_high * high_side
    for i in range(B):
        out_ref[i] = warmth[i] + (solved[i] - gf_x[i] * flux_low + gl_x[i] * flux_high)

    settle(halo, 4, send_sem.at[0])
    settle(co_z, GROUP - 1, send_sem.at[1])
    settle(end_z, GROUP - 1, send_sem.at[2])
    settle(co_x, GROUPS - 1, send_sem.at[3])
    settle(co_r, ROWS - 1, send_sem.at[4])
    settle(end_x, GROUPS - 1, send_sem.at[5])
    settle(end_r, ROWS - 1, send_sem.at[6])


def shards(warmth, factor):
    def vmem(*shape):
        return pltpu.VMEM(shape, jnp.float32)

    scratch = [
        vmem(B, B, NZ),
        vmem(B, B, NZ),
        vmem(B, B, NZ),
        vmem(B * B, NZ),
        vmem(B * B, NZ),
        vmem(B * B, NZ),
        vmem(B * B, NZ),
        vmem(B * B, NZ),
        vmem(4, 2, B, NZ),
        vmem(4, 2, B, NZ),
        vmem(WEIGHTS, 4 * B, NZ),
        vmem(4 * B, NZ),
    ]
    scratch += [vmem(B, B, NZ) for _ in range(8)]
    scratch += [
        vmem(B, B, NZ),
        vmem(GROUP, 3, B, NZ),
        vmem(GROUPS, 3, B, NZ),
        vmem(ROWS, 3, B, NZ),
        vmem(GROUP, 2, B, NZ),
        vmem(GROUPS, 2, B, NZ),
        vmem(ROWS, B, NZ),
        vmem(2, GROUP, B, NZ),
        vmem(2, GROUP, B, NZ),
        vmem(2, GROUP, B, NZ),
        vmem(GROUP + 1, B, NZ),
        vmem(GROUPS + 1, B, NZ),
        vmem(2, B, NZ),
        vmem(2, B, NZ),
        vmem(ROWS + 1, B, NZ),
        vmem(ROWS + 1, B, NZ),
        vmem(ROWS, B, NZ),
        vmem(ROWS, B, NZ),
        vmem(ROWS + 1, B, NZ),
        vmem(ROWS + 1, B, NZ),
        vmem(GROUP + 1, B, NZ),
        vmem(GROUP + 1, B, NZ),
        pltpu.SemaphoreType.DMA((2,)),
        pltpu.SemaphoreType.DMA((7,)),
        pltpu.SemaphoreType.DMA((7,)),
    ]
    return pl.pallas_call(
        kernel,
        out_shape=jax.ShapeDtypeStruct((B, B, NZ), jnp.float32),
        in_specs=[pl.BlockSpec(memory_space=pltpu.HBM)] * 2,
        out_specs=pl.BlockSpec(memory_space=pltpu.VMEM),
        scratch_shapes=scratch,
        compiler_params=pltpu.CompilerParams(
            collective_id=0, has_side_effects=True, vmem_limit_bytes=55040 * 1024
        ),
    )(warmth, factor)


def solution(mesh):
    return jax.shard_map(
        shards,
        mesh=mesh,
        in_specs=(P("row", "col", None), P("row", "col", None)),
        out_specs=P("row", "col", None),
        check_vma=False,
    )
```

```python
import functools

import jax
import jax.numpy as jnp
from jax import lax
from jax.experimental import pallas as pl
from jax.experimental.pallas import tpu as pltpu
from jax.sharding import PartitionSpec as P

MESH = pl.DeviceIdType.MESH
LATERAL = 1500.0
UPRIGHT = 2.0
WARM_WALL = 0.5
CHILL_WALL = -0.5
RESPONSE = 0.4
B = 16
NZ = 128
ROWS = 8
GROUP = 8
GROUPS = 4
STEPS = (1, 2, 4, 8, 16, 32, 64)
WEIGHTS = 19


def inverse(value):
    guess = pl.reciprocal(value, approx=True)
    return guess * (2.0 - value * guess)


def conductivity(temperature, factor):
    return factor * (1.0 + RESPONSE * jnp.tanh(temperature))


def half_resistance(conduct):
    return inverse((2.0 * LATERAL) * conduct)


def block_coefficients(half, link, back, green_first, green_last, out):
    left = jnp.ones((B, NZ), jnp.float32)
    right = jnp.ones((B, NZ), jnp.float32)
    lefts, rights = {}, {}
    for step in range(1, B):
        i, j = step, B - step
        resist = half[i - 1] + half[i]
        lefts[i] = inverse(1.0 + left * resist)
        link[i] = lefts[i]
        back[i] = lefts[i] * resist
        left = 1.0 + left * lefts[i]
        resist = half[j - 1] + half[j]
        rights[j] = inverse(1.0 + right * resist)
        right = 1.0 + right * rights[j]
    first, last = inverse(right), inverse(left)
    out[0] = first + half[0]
    out[1] = last + half[B - 1]
    green_first[0] = first
    green_last[B - 1] = last
    for i in range(1, B):
        first = first * rights[i]
        green_first[i] = first
        last = last * lefts[B - i]
        green_last[B - 1 - i] = last
    out[2] = first


def block_ends(load, green_first, green_last, out):
    firsts = [None] * 4
    lasts = [None] * 4
    for i in range(B):
        value = load(i)
        a, b = green_first[i] * value, green_last[i] * value
        k = i % 4
        firsts[k] = a if firsts[k] is None else firsts[k] + a
        lasts[k] = b if lasts[k] is None else lasts[k] + b
    out[0] = (firsts[0] + firsts[1]) + (firsts[2] + firsts[3])
    out[1] = (lasts[0] + lasts[1]) + (lasts[2] + lasts[3])


def block_solve(load, store, link, back, green_last):
    values = [load(0)]
    for i in range(1, B):
        values.append(load(i) + link[i] * values[-1])
    solved = values[-1] * green_last[B - 1]
    store(B - 1, solved)
    for i in range(B - 1, 0, -1):
        solved = back[i] * values[i - 1] + link[i] * solved
        store(i - 1, solved)


def chain_factors(count, coeffs, link, inv, carry):
    previous = None
    for i in range(1, count):
        pivot = coeffs[i - 1, 1] + coeffs[i, 0]
        if previous is not None:
            link[i] = coeffs[i - 1, 2] * previous
            pivot = pivot - coeffs[i - 1, 2] * link[i]
        previous = inverse(pivot)
        inv[i] = previous
        carry[i] = coeffs[i, 2] * previous


def chain_solve(count, ends, link, inv, carry, out):
    values = [None, ends[1, 0] - ends[0, 1]]
    for i in range(2, count):
        values.append((ends[i, 0] - ends[i - 1, 1]) + link[i] * values[-1])
    flux = values[count - 1] * inv[count - 1]
    out[count - 1] = flux
    for i in range(count - 2, 0, -1):
        flux = values[i] * inv[i] + carry[i] * flux
        out[i] = flux


def two_sided_factors(count, coeffs, left_inv, right_inv, left_link, right_link):
    zero = jnp.zeros((B, NZ), jnp.float32)
    left_inv[0] = zero
    right_inv[count] = zero
    below, above = zero, zero
    for i in range(1, count):
        j = count - i
        left_link[i - 1] = below
        pivot = coeffs[i - 1, 1] + coeffs[i, 0] - coeffs[i - 1, 2] * below
        pivot = inverse(pivot)
        left_inv[i] = pivot
        below = coeffs[i, 2] * pivot
        right_link[j] = above
        pivot = coeffs[j - 1, 1] + coeffs[j, 0] - coeffs[j, 2] * above
        pivot = inverse(pivot)
        right_inv[j] = pivot
        above = coeffs[j - 1, 2] * pivot
    left_link[count - 1] = below
    right_link[0] = above


def sweep_sides(count, parts, left_link, right_link, from_low, from_high):
    zero = jnp.zeros((B, NZ), jnp.float32)
    from_low[0] = zero
    from_high[count] = zero
    low, high = parts[0], parts[count - 1]
    from_low[1] = low
    from_high[count - 1] = high
    for i in range(1, count - 1):
        low = parts[i] + left_link[i] * low
        from_low[i + 1] = low
        high = parts[count - 1 - i] + right_link[count - 1 - i] * high
        from_high[count - 1 - i] = high


def group_coefficients(coeffs, link, inv, carry, from_left, from_right, out):
    n = GROUP
    zero = jnp.zeros((B, NZ), jnp.float32)
    one = jnp.ones((B, NZ), jnp.float32)
    flux = carry[n - 1]
    from_right[n] = one
    from_right[0] = zero
    from_right[n - 1] = flux
    out[1] = coeffs[n - 1, 1] - coeffs[n - 1, 2] * flux
    for i in range(n - 2, 0, -1):
        flux = carry[i] * flux
        from_right[i] = flux
    out[2] = coeffs[0, 2] * flux
    values = [None, coeffs[0, 2]]
    for i in range(2, n):
        values.append(link[i] * values[-1])
    flux = values[n - 1] * inv[n - 1]
    from_left[0] = one
    from_left[n] = zero
    from_left[n - 1] = flux
    for i in range(n - 2, 0, -1):
        flux = values[i] * inv[i] + carry[i] * flux
        from_left[i] = flux
    out[0] = coeffs[0, 0] - coeffs[0, 2] * flux


def up(value, stride):
    return pltpu.roll(value, stride, axis=1)


def down(value, stride):
    return pltpu.roll(value, NZ - stride, axis=1)


def upright_bands(conduct):
    lane = lax.broadcasted_iota(jnp.int32, conduct.shape, 1)
    below = up(conduct, 1)
    face = (2.0 * conduct * below) * inverse(conduct + below)
    inner = jnp.where(lane == 0, 0.0, UPRIGHT * face)
    wall = jnp.where((lane == 0) | (lane == NZ - 1), UPRIGHT * conduct, 0.0)
    main = 1.0 + inner + down(inner, 1) + wall
    return inner, main


def upright_step(link, main, stride):
    inv = inverse(main)
    low = link * up(inv, stride)
    high = link * inv
    new_main = main - low * link - down(high * link, stride)
    return low, high, low * up(link, stride), new_main


def kernel(
    warmth_hbm,
    factor_hbm,
    out_ref,
    warmth,
    factor,
    half_x,
    warmth_t,
    conduct_t,
    half_y,
    side_t,
    side_n,
    halo,
    edges,
    weights,
    scale_f,
    link_x,
    back_x,
    gf_x,
    gl_x,
    link_y,
    back_y,
    gf_y,
    gl_y,
    solved,
    co_z,
    co_x,
    co_r,
    end_z,
    end_x,
    end_r,
    ch_link,
    ch_inv,
    ch_carry,
    flux_z,
    flux_x,
    ends,
    parts,
    left_inv,
    right_inv,
    left_link,
    right_link,
    from_low,
    from_high,
    from_left,
    from_right,
    load_sem,
    send_sem,
    recv_sem,
):
    row = lax.axis_index("row")
    col = lax.axis_index("col")
    me_x = col // GROUP
    me_z = lax.rem(col, GROUP)
    base = me_x * GROUP

    far_first = (4, 3, 5, 2, 6, 1, 7)
    z_peers = [(row, base + lax.rem(me_z + k, GROUP)) for k in far_first]
    x_peers = [(row, lax.rem(col + GROUP * k, GROUP * GROUPS)) for k in (2, 1, 3)]
    row_peers = [(lax.rem(row + k, ROWS), col) for k in far_first]
    columns = GROUP * GROUPS
    row_up, row_down = (lax.rem(row + 1, ROWS), col), (lax.rem(row + ROWS - 1, ROWS), col)
    col_up, col_down = (row, lax.rem(col + 1, columns)), (row, lax.rem(col + columns - 1, columns))

    barrier = pltpu.get_barrier_semaphore()
    everyone = [col_up, col_down] + row_peers + z_peers + x_peers
    for peer in everyone:
        pl.semaphore_signal(barrier, inc=1, device_id=peer, device_id_type=MESH)
    load_w = pltpu.make_async_copy(warmth_hbm, warmth, load_sem.at[0])
    load_f = pltpu.make_async_copy(factor_hbm, factor, load_sem.at[1])
    load_w.start()
    load_f.start()
    load_w.wait()
    load_f.wait()
    for k, array in enumerate((warmth, factor)):
        edges[0, k] = array[B - 1]
        edges[1, k] = array[0]
        edges[2, k] = array[:, B - 1, :]
        edges[3, k] = array[:, 0, :]

    def remote(src, dst, which, peer):
        return pltpu.make_async_remote_copy(
            src_ref=src,
            dst_ref=dst,
            send_sem=send_sem.at[which],
            recv_sem=recv_sem.at[which],
            device_id=peer,
            device_id_type=MESH,
        )

    pl.semaphore_wait(barrier, len(everyone))
    for k, peer in ((2, col_up), (3, col_down), (0, row_up), (1, row_down)):
        remote(edges.at[k], halo.at[k], 0, peer).start()

    def settle(buffer, count, sem):
        view = buffer.at[pl.ds(0, count)]
        pltpu.make_async_copy(view, view, sem).wait()

    def spread(buffer, index, which, peers):
        for peer in peers:
            remote(buffer.at[index], buffer.at[index], which, peer).start()


    before = None
    for i in range(B):
        w = warmth[i]
        c = conductivity(w, factor[i])
        h = half_resistance(c)
        half_x[i] = h
        warmth_t[pl.ds(i, B, stride=B), :] = w
        conduct_t[pl.ds(i, B, stride=B), :] = c
        half_y[pl.ds(i, B, stride=B), :] = h
        if before is None:
            edge_low_c = c
            flux_low = None
        else:
            flux_high = inverse(before[1] + h) * (w - before[0])
            gain = flux_high if flux_low is None else flux_high - flux_low
            side_t[pl.ds(i - 1, B, stride=B), :] = gain
            flux_low = flux_high
        before = (w, h)
    side_t[pl.ds(B - 1, B, stride=B), :] = -flux_low
    edge_high_c = c

    class Rows:
        def __init__(self, ref):
            self.ref = ref

        def __getitem__(self, i):
            return self.ref[i * B : (i + 1) * B, :]

    half_rows = Rows(half_y)
    block_coefficients(half_rows, link_y, back_y, gf_y, gl_y, co_z.at[me_z])
    spread(co_z, me_z, 1, z_peers[::-1])

    flux_low = None
    for i in range(B):
        if i < B - 1:
            flux_high = inverse(half_rows[i] + half_rows[i + 1]) * (
                warmth_t[(i + 1) * B : (i + 2) * B, :] - warmth_t[i * B : (i + 1) * B, :]
            )
        gain = flux_high if i == 0 else (-flux_low if i == B - 1 else flux_high - flux_low)
        side_t[i * B : (i + 1) * B, :] = side_t[i * B : (i + 1) * B, :] + gain
        flux_low = flux_high

    cells, last = B * B, B * (B - 1)
    lane = lax.broadcasted_iota(jnp.int32, (cells, NZ), 1)
    w = warmth_t[...]
    c = conduct_t[...]
    link, main = upright_bands(jnp.concatenate([c, edge_low_c, edge_high_c], axis=0))
    flux = jnp.where(lane == 0, UPRIGHT * c * (w - WARM_WALL), link[0:cells] * (w - up(w, 1)))
    flux_above = jnp.where(lane == NZ - 1, UPRIGHT * c * (CHILL_WALL - w), down(flux, 1))
    side = 2.0 * (side_t[...] + (flux_above - flux))

    def faces(value):
        return jnp.concatenate(
            [value[cells : cells + 2 * B], value[0:B], value[last : last + B]], axis=0
        )

    lows, highs = [], []
    for stride in STEPS:
        low, high, link, main = upright_step(link, main, stride)
        side = side + low[0:cells] * up(side, stride) + down(high[0:cells] * side, stride)
        lows.append(faces(low))
        highs.append(down(faces(high), stride))
    inv = inverse(main)
    side_t[...] = side * inv[0:cells]
    scale_f[...] = faces(inv)
    for n in range(0, len(STEPS) - 1, 2):
        wide = STEPS[n + 1]
        weights[3 * n] = lows[n] + lows[n + 1] * up(highs[n], wide)
        weights[3 * n + 1] = highs[n] + highs[n + 1] * down(lows[n], wide)
        weights[3 * n + 2] = lows[n + 1]
        weights[3 * n + 3] = highs[n + 1]
        weights[3 * n + 4] = lows[n + 1] * up(lows[n], wide)
        weights[3 * n + 5] = highs[n + 1] * down(highs[n], wide)
    weights[WEIGHTS - 1] = lows[-1] + highs[-1]

    settle(halo, 4, recv_sem.at[0])

    def through(near_w, near_h, k, present):
        other = halo[k, 0]
        resist = near_h + half_resistance(conductivity(other, halo[k, 1]))
        return (2.0 * present) * (inverse(resist) * (other - near_w))

    def flag(condition):
        return jnp.where(condition, 1.0, 0.0).astype(jnp.float32)

    share = jnp.concatenate(
        [
            through(warmth[0], half_x[0], 0, flag(row > 0)),
            through(warmth[B - 1], half_x[B - 1], 1, flag(row < ROWS - 1)),
            through(warmth_t[0:B, :], half_rows[0], 2, flag(col > 0)),
            through(warmth_t[last : last + B, :], half_rows[B - 1], 3, flag(col < columns - 1)),
        ],
        axis=0,
    )
    for n in range(0, len(STEPS) - 1, 2):
        stride = STEPS[n]
        share = (
            (share + weights[3 * n] * up(share, stride))
            + (weights[3 * n + 1] * down(share, stride) + weights[3 * n + 2] * up(share, 2 * stride))
            + (weights[3 * n + 3] * down(share, 2 * stride) + weights[3 * n + 4] * up(share, 3 * stride))
            + weights[3 * n + 5] * down(share, 3 * stride)
        )
    share = (share + weights[WEIGHTS - 1] * up(share, STEPS[-1])) * scale_f[...]
    side_t[0:B, :] = side_t[0:B, :] + share[2 * B : 3 * B]
    side_t[last : last + B, :] = side_t[last : last + B, :] + share[3 * B : 4 * B]
    side_t[pl.ds(0, B, stride=B), :] = side_t[pl.ds(0, B, stride=B), :] + share[0:B]
    side_t[pl.ds(B - 1, B, stride=B), :] = side_t[pl.ds(B - 1, B, stride=B), :] + share[B : 2 * B]

    side_rows = Rows(side_t)
    block_ends(lambda i: side_rows[i], gf_y, gl_y, end_z.at[me_z])
    spread(end_z, me_z, 2, z_peers)

    settle(co_z, GROUP - 1, recv_sem.at[1])
    chain_factors(GROUP, co_z, ch_link.at[0], ch_inv.at[0], ch_carry.at[0])
    group_coefficients(
        co_z, ch_link.at[0], ch_inv.at[0], ch_carry.at[0], from_left, from_right, co_x.at[me_x]
    )
    spread(co_x, me_x, 3, x_peers)
    block_coefficients(half_x, link_x, back_x, gf_x, gl_x, co_r.at[row])
    spread(co_r, row, 4, row_peers[::-1])

    def keep(i, value):
        solved[i] = value

    block_solve(lambda i: side_rows[i], keep, link_y, back_y, gl_y)
    zero = jnp.zeros((B, NZ), jnp.float32)
    for ref, count in ((flux_z, GROUP), (flux_x, GROUPS)):
        ref[0] = zero
        ref[count] = zero

    settle(end_z, GROUP - 1, recv_sem.at[2])
    chain_solve(GROUP, end_z, ch_link.at[0], ch_inv.at[0], ch_carry.at[0], flux_z)
    end_x[me_x, 0] = end_z[0, 0] + co_z[0, 2] * flux_z[1]
    end_x[me_x, 1] = end_z[GROUP - 1, 1] - co_z[GROUP - 1, 2] * flux_z[GROUP - 1]
    spread(end_x, me_x, 5, x_peers)

    settle(co_x, GROUPS - 1, recv_sem.at[3])
    chain_factors(GROUPS, co_x, ch_link.at[1], ch_inv.at[1], ch_carry.at[1])
    settle(co_r, ROWS - 1, recv_sem.at[4])
    two_sided_factors(ROWS, co_r, left_inv, right_inv, left_link, right_link)
    own_left, own_right, own_link = left_inv[row], right_inv[row + 1], co_r[row, 2]
    to_high = own_link * own_left
    to_low = own_link * own_right
    weight_high = own_right * inverse(1.0 - to_high * to_low)
    weight_cross = to_high * weight_high
    weight_low = own_left * (1.0 + own_link * weight_cross)

    settle(end_x, GROUPS - 1, recv_sem.at[5])
    chain_solve(GROUPS, end_x, ch_link.at[1], ch_inv.at[1], ch_carry.at[1], flux_x)
    outer_low, outer_high = flux_x[me_x], flux_x[me_x + 1]

    def inner_flux(i):
        return flux_z[i] + from_left[i] * outer_low + from_right[i] * outer_high

    flux_low, flux_high = inner_flux(me_z), inner_flux(me_z + 1)
    for i in range(B):
        side_n[pl.ds(i, B, stride=B), :] = solved[i] - gf_y[i] * flux_low + gl_y[i] * flux_high

    section = Rows(side_n)
    block_ends(lambda i: section[i], gf_x, gl_x, ends)
    own_first, own_last = ends[0], ends[1]
    parts[0] = to_high * own_first - own_last
    parts[1] = own_first - to_low * own_last
    end_r[row] = own_first
    for peer in row_peers:
        side = jnp.where(peer[0] > row, 0, 1)
        remote(parts.at[side], end_r.at[row], 6, peer).start()
    block_solve(lambda i: section[i], keep, link_x, back_x, gl_x)

    settle(end_r, ROWS - 1, recv_sem.at[6])
    sweep_sides(ROWS, end_r, left_link, right_link, from_low, from_high)
    low_side = own_first + from_low[row]
    high_side = from_high[row + 1] - own_last
    flux_low = weight_low * low_side + weight_cross * high_side
    flux_high = weight_cross * low_side + weight_high * high_side
    for i in range(B):
        out_ref[i] = warmth[i] + (solved[i] - gf_x[i] * flux_low + gl_x[i] * flux_high)

    settle(halo, 4, send_sem.at[0])
    settle(co_z, GROUP - 1, send_sem.at[1])
    settle(end_z, GROUP - 1, send_sem.at[2])
    settle(co_x, GROUPS - 1, send_sem.at[3])
    settle(co_r, ROWS - 1, send_sem.at[4])
    settle(end_x, GROUPS - 1, send_sem.at[5])
    settle(end_r, ROWS - 1, send_sem.at[6])


def shards(warmth, factor):
    def vmem(*shape):
        return pltpu.VMEM(shape, jnp.float32)

    scratch = [
        vmem(B, B, NZ),
        vmem(B, B, NZ),
        vmem(B, B, NZ),
        vmem(B * B, NZ),
        vmem(B * B, NZ),
        vmem(B * B, NZ),
        vmem(B * B, NZ),
        vmem(B * B, NZ),
        vmem(4, 2, B, NZ),
        vmem(4, 2, B, NZ),
        vmem(WEIGHTS, 4 * B, NZ),
        vmem(4 * B, NZ),
    ]
    scratch += [vmem(B, B, NZ) for _ in range(8)]
    scratch += [
        vmem(B, B, NZ),
        vmem(GROUP, 3, B, NZ),
        vmem(GROUPS, 3, B, NZ),
        vmem(ROWS, 3, B, NZ),
        vmem(GROUP, 2, B, NZ),
        vmem(GROUPS, 2, B, NZ),
        vmem(ROWS, B, NZ),
        vmem(2, GROUP, B, NZ),
        vmem(2, GROUP, B, NZ),
        vmem(2, GROUP, B, NZ),
        vmem(GROUP + 1, B, NZ),
        vmem(GROUPS + 1, B, NZ),
        vmem(2, B, NZ),
        vmem(2, B, NZ),
        vmem(ROWS + 1, B, NZ),
        vmem(ROWS + 1, B, NZ),
        vmem(ROWS, B, NZ),
        vmem(ROWS, B, NZ),
        vmem(ROWS + 1, B, NZ),
        vmem(ROWS + 1, B, NZ),
        vmem(GROUP + 1, B, NZ),
        vmem(GROUP + 1, B, NZ),
        pltpu.SemaphoreType.DMA((2,)),
        pltpu.SemaphoreType.DMA((7,)),
        pltpu.SemaphoreType.DMA((7,)),
    ]
    return pl.pallas_call(
        kernel,
        out_shape=jax.ShapeDtypeStruct((B, B, NZ), jnp.float32),
        in_specs=[pl.BlockSpec(memory_space=pltpu.HBM)] * 2,
        out_specs=pl.BlockSpec(memory_space=pltpu.VMEM),
        scratch_shapes=scratch,
        compiler_params=pltpu.CompilerParams(
            collective_id=0, has_side_effects=True, vmem_limit_bytes=55040 * 1024
        ),
    )(warmth, factor)


def solution(mesh):
    return jax.shard_map(
        shards,
        mesh=mesh,
        in_specs=(P("row", "col", None), P("row", "col", None)),
        out_specs=P("row", "col", None),
        check_vma=False,
    )
```

```python
import functools

import jax
import jax.numpy as jnp
from jax import lax
from jax.experimental import pallas as pl
from jax.experimental.pallas import tpu as pltpu
from jax.sharding import PartitionSpec as P

MESH = pl.DeviceIdType.MESH
LATERAL = 1500.0
UPRIGHT = 2.0
WARM_WALL = 0.5
CHILL_WALL = -0.5
RESPONSE = 0.4
B = 16
NZ = 128
ROWS = 8
GROUP = 8
GROUPS = 4
STEPS = (1, 2, 4, 8, 16, 32, 64)
WEIGHTS = 19


def inverse(value):
    guess = pl.reciprocal(value, approx=True)
    return guess * (2.0 - value * guess)


def conductivity(temperature, factor):
    return factor * (1.0 + RESPONSE * jnp.tanh(temperature))


def half_resistance(conduct):
    return inverse((2.0 * LATERAL) * conduct)


def block_coefficients(half, link, back, green_first, green_last, out):
    left = jnp.ones((B, NZ), jnp.float32)
    right = jnp.ones((B, NZ), jnp.float32)
    lefts, rights = {}, {}
    for step in range(1, B):
        i, j = step, B - step
        resist = half[i - 1] + half[i]
        lefts[i] = inverse(1.0 + left * resist)
        link[i] = lefts[i]
        back[i] = lefts[i] * resist
        left = 1.0 + left * lefts[i]
        resist = half[j - 1] + half[j]
        rights[j] = inverse(1.0 + right * resist)
        right = 1.0 + right * rights[j]
    first, last = inverse(right), inverse(left)
    out[0] = first + half[0]
    out[1] = last + half[B - 1]
    green_first[0] = first
    green_last[B - 1] = last
    for i in range(1, B):
        first = first * rights[i]
        green_first[i] = first
        last = last * lefts[B - i]
        green_last[B - 1 - i] = last
    out[2] = first


def block_ends(load, green_first, green_last, out):
    firsts = [None] * 4
    lasts = [None] * 4
    for i in range(B):
        value = load(i)
        a, b = green_first[i] * value, green_last[i] * value
        k = i % 4
        firsts[k] = a if firsts[k] is None else firsts[k] + a
        lasts[k] = b if lasts[k] is None else lasts[k] + b
    out[0] = (firsts[0] + firsts[1]) + (firsts[2] + firsts[3])
    out[1] = (lasts[0] + lasts[1]) + (lasts[2] + lasts[3])


def block_solve(load, store, link, back, green_last):
    values = [load(0)]
    for i in range(1, B):
        values.append(load(i) + link[i] * values[-1])
    solved = values[-1] * green_last[B - 1]
    store(B - 1, solved)
    for i in range(B - 1, 0, -1):
        solved = back[i] * values[i - 1] + link[i] * solved
        store(i - 1, solved)


def chain_factors(count, coeffs, link, inv, carry):
    previous = None
    for i in range(1, count):
        pivot = coeffs[i - 1, 1] + coeffs[i, 0]
        if previous is not None:
            link[i] = coeffs[i - 1, 2] * previous
            pivot = pivot - coeffs[i - 1, 2] * link[i]
        previous = inverse(pivot)
        inv[i] = previous
        carry[i] = coeffs[i, 2] * previous


def chain_solve(count, ends, link, inv, carry, out):
    values = [None, ends[1, 0] - ends[0, 1]]
    for i in range(2, count):
        values.append((ends[i, 0] - ends[i - 1, 1]) + link[i] * values[-1])
    flux = values[count - 1] * inv[count - 1]
    out[count - 1] = flux
    for i in range(count - 2, 0, -1):
        flux = values[i] * inv[i] + carry[i] * flux
        out[i] = flux


def two_sided_factors(count, coeffs, left_inv, right_inv, left_link, right_link):
    zero = jnp.zeros((B, NZ), jnp.float32)
    left_inv[0] = zero
    right_inv[count] = zero
    below, above = zero, zero
    for i in range(1, count):
        j = count - i
        left_link[i - 1] = below
        pivot = coeffs[i - 1, 1] + coeffs[i, 0] - coeffs[i - 1, 2] * below
        pivot = inverse(pivot)
        left_inv[i] = pivot
        below = coeffs[i, 2] * pivot
        right_link[j] = above
        pivot = coeffs[j - 1, 1] + coeffs[j, 0] - coeffs[j, 2] * above
        pivot = inverse(pivot)
        right_inv[j] = pivot
        above = coeffs[j - 1, 2] * pivot
    left_link[count - 1] = below
    right_link[0] = above


def sweep_sides(count, parts, left_link, right_link, from_low, from_high):
    zero = jnp.zeros((B, NZ), jnp.float32)
    from_low[0] = zero
    from_high[count] = zero
    low, high = parts[0], parts[count - 1]
    from_low[1] = low
    from_high[count - 1] = high
    for i in range(1, count - 1):
        low = parts[i] + left_link[i] * low
        from_low[i + 1] = low
        high = parts[count - 1 - i] + right_link[count - 1 - i] * high
        from_high[count - 1 - i] = high


def group_coefficients(coeffs, link, inv, carry, from_left, from_right, out):
    n = GROUP
    zero = jnp.zeros((B, NZ), jnp.float32)
    one = jnp.ones((B, NZ), jnp.float32)
    flux = carry[n - 1]
    from_right[n] = one
    from_right[0] = zero
    from_right[n - 1] = flux
    out[1] = coeffs[n - 1, 1] - coeffs[n - 1, 2] * flux
    for i in range(n - 2, 0, -1):
        flux = carry[i] * flux
        from_right[i] = flux
    out[2] = coeffs[0, 2] * flux
    values = [None, coeffs[0, 2]]
    for i in range(2, n):
        values.append(link[i] * values[-1])
    flux = values[n - 1] * inv[n - 1]
    from_left[0] = one
    from_left[n] = zero
    from_left[n - 1] = flux
    for i in range(n - 2, 0, -1):
        flux = values[i] * inv[i] + carry[i] * flux
        from_left[i] = flux
    out[0] = coeffs[0, 0] - coeffs[0, 2] * flux


def up(value, stride):
    return pltpu.roll(value, stride, axis=1)


def down(value, stride):
    return pltpu.roll(value, NZ - stride, axis=1)


def upright_bands(conduct):
    lane = lax.broadcasted_iota(jnp.int32, conduct.shape, 1)
    below = up(conduct, 1)
    face = (2.0 * conduct * below) * inverse(conduct + below)
    inner = jnp.where(lane == 0, 0.0, UPRIGHT * face)
    wall = jnp.where((lane == 0) | (lane == NZ - 1), UPRIGHT * conduct, 0.0)
    main = 1.0 + inner + down(inner, 1) + wall
    return inner, main


def upright_step(link, main, stride):
    inv = inverse(main)
    low = link * up(inv, stride)
    high = link * inv
    new_main = main - low * link - down(high * link, stride)
    return low, high, low * up(link, stride), new_main


def kernel(
    warmth_hbm,
    factor_hbm,
    out_ref,
    warmth,
    factor,
    half_x,
    warmth_t,
    conduct_t,
    half_y,
    side_t,
    side_n,
    halo,
    edges,
    weights,
    scale_f,
    link_x,
    back_x,
    gf_x,
    gl_x,
    link_y,
    back_y,
    gf_y,
    gl_y,
    solved,
    co_z,
    co_x,
    co_r,
    end_z,
    end_x,
    end_r,
    ch_link,
    ch_inv,
    ch_carry,
    flux_z,
    flux_x,
    ends,
    parts,
    left_inv,
    right_inv,
    left_link,
    right_link,
    from_low,
    from_high,
    from_left,
    from_right,
    load_sem,
    send_sem,
    recv_sem,
):
    row = lax.axis_index("row")
    col = lax.axis_index("col")
    me_x = col // GROUP
    me_z = lax.rem(col, GROUP)
    base = me_x * GROUP

    far_first = (4, 3, 5, 2, 6, 1, 7)
    z_peers = [(row, base + lax.rem(me_z + k, GROUP)) for k in far_first]
    x_peers = [(row, lax.rem(col + GROUP * k, GROUP * GROUPS)) for k in (2, 1, 3)]
    row_peers = [(lax.rem(row + k, ROWS), col) for k in far_first]
    columns = GROUP * GROUPS
    row_up, row_down = (lax.rem(row + 1, ROWS), col), (lax.rem(row + ROWS - 1, ROWS), col)
    col_up, col_down = (row, lax.rem(col + 1, columns)), (row, lax.rem(col + columns - 1, columns))

    load_w = pltpu.make_async_copy(warmth_hbm, warmth, load_sem.at[0])
    load_f = pltpu.make_async_copy(factor_hbm, factor, load_sem.at[1])
    load_w.start()
    load_f.start()
    barrier = pltpu.get_barrier_semaphore()
    everyone = [col_up, col_down] + row_peers + z_peers + x_peers
    for peer in everyone:
        pl.semaphore_signal(barrier, inc=1, device_id=peer, device_id_type=MESH)
    load_w.wait()
    load_f.wait()
    for k, array in enumerate((warmth, factor)):
        edges[0, k] = array[B - 1]
        edges[1, k] = array[0]
        edges[2, k] = array[:, B - 1, :]
        edges[3, k] = array[:, 0, :]

    def remote(src, dst, which, peer):
        return pltpu.make_async_remote_copy(
            src_ref=src,
            dst_ref=dst,
            send_sem=send_sem.at[which],
            recv_sem=recv_sem.at[which],
            device_id=peer,
            device_id_type=MESH,
        )

    pl.semaphore_wait(barrier, len(everyone))
    for k, peer in ((2, col_up), (3, col_down), (0, row_up), (1, row_down)):
        remote(edges.at[k], halo.at[k], 0, peer).start()

    def settle(buffer, count, sem):
        view = buffer.at[pl.ds(0, count)]
        pltpu.make_async_copy(view, view, sem).wait()

    def spread(buffer, index, which, peers):
        for peer in peers:
            remote(buffer.at[index], buffer.at[index], which, peer).start()


    before = None
    for i in range(B):
        w = warmth[i]
        c = conductivity(w, factor[i])
        h = half_resistance(c)
        half_x[i] = h
        warmth_t[pl.ds(i, B, stride=B), :] = w
        conduct_t[pl.ds(i, B, stride=B), :] = c
        half_y[pl.ds(i, B, stride=B), :] = h
        if before is None:
            edge_low_c = c
            flux_low = None
        else:
            flux_high = inverse(before[1] + h) * (w - before[0])
            gain = flux_high if flux_low is None else flux_high - flux_low
            side_t[pl.ds(i - 1, B, stride=B), :] = gain
            flux_low = flux_high
        before = (w, h)
    side_t[pl.ds(B - 1, B, stride=B), :] = -flux_low
    edge_high_c = c

    class Rows:
        def __init__(self, ref):
            self.ref = ref

        def __getitem__(self, i):
            return self.ref[i * B : (i + 1) * B, :]

    half_rows = Rows(half_y)
    block_coefficients(half_rows, link_y, back_y, gf_y, gl_y, co_z.at[me_z])
    spread(co_z, me_z, 1, z_peers[::-1])

    flux_low = None
    for i in range(B):
        if i < B - 1:
            flux_high = inverse(half_rows[i] + half_rows[i + 1]) * (
                warmth_t[(i + 1) * B : (i + 2) * B, :] - warmth_t[i * B : (i + 1) * B, :]
            )
        gain = flux_high if i == 0 else (-flux_low if i == B - 1 else flux_high - flux_low)
        side_t[i * B : (i + 1) * B, :] = side_t[i * B : (i + 1) * B, :] + gain
        flux_low = flux_high

    cells, last = B * B, B * (B - 1)
    lane = lax.broadcasted_iota(jnp.int32, (cells, NZ), 1)
    w = warmth_t[...]
    c = conduct_t[...]
    link, main = upright_bands(jnp.concatenate([c, edge_low_c, edge_high_c], axis=0))
    flux = jnp.where(lane == 0, UPRIGHT * c * (w - WARM_WALL), link[0:cells] * (w - up(w, 1)))
    flux_above = jnp.where(lane == NZ - 1, UPRIGHT * c * (CHILL_WALL - w), down(flux, 1))
    side = 2.0 * (side_t[...] + (flux_above - flux))

    def faces(value):
        return jnp.concatenate(
            [value[cells : cells + 2 * B], value[0:B], value[last : last + B]], axis=0
        )

    lows, highs = [], []
    for stride in STEPS:
        low, high, link, main = upright_step(link, main, stride)
        side = side + low[0:cells] * up(side, stride) + down(high[0:cells] * side, stride)
        lows.append(faces(low))
        highs.append(down(faces(high), stride))
    inv = inverse(main)
    side_t[...] = side * inv[0:cells]
    scale_f[...] = faces(inv)
    for n in range(0, len(STEPS) - 1, 2):
        wide = STEPS[n + 1]
        weights[3 * n] = lows[n] + lows[n + 1] * up(highs[n], wide)
        weights[3 * n + 1] = highs[n] + highs[n + 1] * down(lows[n], wide)
        weights[3 * n + 2] = lows[n + 1]
        weights[3 * n + 3] = highs[n + 1]
        weights[3 * n + 4] = lows[n + 1] * up(lows[n], wide)
        weights[3 * n + 5] = highs[n + 1] * down(highs[n], wide)
    weights[WEIGHTS - 1] = lows[-1] + highs[-1]

    settle(halo, 4, recv_sem.at[0])

    def through(near_w, near_h, k, present):
        other = halo[k, 0]
        resist = near_h + half_resistance(conductivity(other, halo[k, 1]))
        return (2.0 * present) * (inverse(resist) * (other - near_w))

    def flag(condition):
        return jnp.where(condition, 1.0, 0.0).astype(jnp.float32)

    share = jnp.concatenate(
        [
            through(warmth[0], half_x[0], 0, flag(row > 0)),
            through(warmth[B - 1], half_x[B - 1], 1, flag(row < ROWS - 1)),
            through(warmth_t[0:B, :], half_rows[0], 2, flag(col > 0)),
            through(warmth_t[last : last + B, :], half_rows[B - 1], 3, flag(col < columns - 1)),
        ],
        axis=0,
    )
    for n in range(0, len(STEPS) - 1, 2):
        stride = STEPS[n]
        share = (
            (share + weights[3 * n] * up(share, stride))
            + (weights[3 * n + 1] * down(share, stride) + weights[3 * n + 2] * up(share, 2 * stride))
            + (weights[3 * n + 3] * down(share, 2 * stride) + weights[3 * n + 4] * up(share, 3 * stride))
            + weights[3 * n + 5] * down(share, 3 * stride)
        )
    share = (share + weights[WEIGHTS - 1] * up(share, STEPS[-1])) * scale_f[...]
    side_t[0:B, :] = side_t[0:B, :] + share[2 * B : 3 * B]
    side_t[last : last + B, :] = side_t[last : last + B, :] + share[3 * B : 4 * B]
    side_t[pl.ds(0, B, stride=B), :] = side_t[pl.ds(0, B, stride=B), :] + share[0:B]
    side_t[pl.ds(B - 1, B, stride=B), :] = side_t[pl.ds(B - 1, B, stride=B), :] + share[B : 2 * B]

    side_rows = Rows(side_t)
    block_ends(lambda i: side_rows[i], gf_y, gl_y, end_z.at[me_z])
    spread(end_z, me_z, 2, z_peers)

    settle(co_z, GROUP - 1, recv_sem.at[1])
    chain_factors(GROUP, co_z, ch_link.at[0], ch_inv.at[0], ch_carry.at[0])
    group_coefficients(
        co_z, ch_link.at[0], ch_inv.at[0], ch_carry.at[0], from_left, from_right, co_x.at[me_x]
    )
    spread(co_x, me_x, 3, x_peers)
    block_coefficients(half_x, link_x, back_x, gf_x, gl_x, co_r.at[row])
    spread(co_r, row, 4, row_peers[::-1])

    def keep(i, value):
        solved[i] = value

    block_solve(lambda i: side_rows[i], keep, link_y, back_y, gl_y)
    zero = jnp.zeros((B, NZ), jnp.float32)
    for ref, count in ((flux_z, GROUP), (flux_x, GROUPS)):
        ref[0] = zero
        ref[count] = zero

    settle(end_z, GROUP - 1, recv_sem.at[2])
    chain_solve(GROUP, end_z, ch_link.at[0], ch_inv.at[0], ch_carry.at[0], flux_z)
    end_x[me_x, 0] = end_z[0, 0] + co_z[0, 2] * flux_z[1]
    end_x[me_x, 1] = end_z[GROUP - 1, 1] - co_z[GROUP - 1, 2] * flux_z[GROUP - 1]
    spread(end_x, me_x, 5, x_peers)

    settle(co_x, GROUPS - 1, recv_sem.at[3])
    chain_factors(GROUPS, co_x, ch_link.at[1], ch_inv.at[1], ch_carry.at[1])
    settle(co_r, ROWS - 1, recv_sem.at[4])
    two_sided_factors(ROWS, co_r, left_inv, right_inv, left_link, right_link)
    own_left, own_right, own_link = left_inv[row], right_inv[row + 1], co_r[row, 2]
    to_high = own_link * own_left
    to_low = own_link * own_right
    weight_high = own_right * inverse(1.0 - to_high * to_low)
    weight_cross = to_high * weight_high
    weight_low = own_left * (1.0 + own_link * weight_cross)

    settle(end_x, GROUPS - 1, recv_sem.at[5])
    chain_solve(GROUPS, end_x, ch_link.at[1], ch_inv.at[1], ch_carry.at[1], flux_x)
    outer_low, outer_high = flux_x[me_x], flux_x[me_x + 1]

    def inner_flux(i):
        return flux_z[i] + from_left[i] * outer_low + from_right[i] * outer_high

    flux_low, flux_high = inner_flux(me_z), inner_flux(me_z + 1)
    for i in range(B):
        side_n[pl.ds(i, B, stride=B), :] = solved[i] - gf_y[i] * flux_low + gl_y[i] * flux_high

    section = Rows(side_n)
    block_ends(lambda i: section[i], gf_x, gl_x, ends)
    own_first, own_last = ends[0], ends[1]
    parts[0] = to_high * own_first - own_last
    parts[1] = own_first - to_low * own_last
    end_r[row] = own_first
    for peer in row_peers:
        side = jnp.where(peer[0] > row, 0, 1)
        remote(parts.at[side], end_r.at[row], 6, peer).start()
    block_solve(lambda i: section[i], keep, link_x, back_x, gl_x)

    settle(end_r, ROWS - 1, recv_sem.at[6])
    sweep_sides(ROWS, end_r, left_link, right_link, from_low, from_high)
    low_side = own_first + from_low[row]
    high_side = from_high[row + 1] - own_last
    flux_low = weight_low * low_side + weight_cross * high_side
    flux_high = weight_cross * low_side + weight_high * high_side
    for i in range(B):
        out_ref[i] = warmth[i] + (solved[i] - gf_x[i] * flux_low + gl_x[i] * flux_high)

    settle(halo, 4, send_sem.at[0])
    settle(co_z, GROUP - 1, send_sem.at[1])
    settle(end_z, GROUP - 1, send_sem.at[2])
    settle(co_x, GROUPS - 1, send_sem.at[3])
    settle(co_r, ROWS - 1, send_sem.at[4])
    settle(end_x, GROUPS - 1, send_sem.at[5])
    settle(end_r, ROWS - 1, send_sem.at[6])


def shards(warmth, factor):
    def vmem(*shape):
        return pltpu.VMEM(shape, jnp.float32)

    scratch = [
        vmem(B, B, NZ),
        vmem(B, B, NZ),
        vmem(B, B, NZ),
        vmem(B * B, NZ),
        vmem(B * B, NZ),
        vmem(B * B, NZ),
        vmem(B * B, NZ),
        vmem(B * B, NZ),
        vmem(4, 2, B, NZ),
        vmem(4, 2, B, NZ),
        vmem(WEIGHTS, 4 * B, NZ),
        vmem(4 * B, NZ),
    ]
    scratch += [vmem(B, B, NZ) for _ in range(8)]
    scratch += [
        vmem(B, B, NZ),
        vmem(GROUP, 3, B, NZ),
        vmem(GROUPS, 3, B, NZ),
        vmem(ROWS, 3, B, NZ),
        vmem(GROUP, 2, B, NZ),
        vmem(GROUPS, 2, B, NZ),
        vmem(ROWS, B, NZ),
        vmem(2, GROUP, B, NZ),
        vmem(2, GROUP, B, NZ),
        vmem(2, GROUP, B, NZ),
        vmem(GROUP + 1, B, NZ),
        vmem(GROUPS + 1, B, NZ),
        vmem(2, B, NZ),
        vmem(2, B, NZ),
        vmem(ROWS + 1, B, NZ),
        vmem(ROWS + 1, B, NZ),
        vmem(ROWS, B, NZ),
        vmem(ROWS, B, NZ),
        vmem(ROWS + 1, B, NZ),
        vmem(ROWS + 1, B, NZ),
        vmem(GROUP + 1, B, NZ),
        vmem(GROUP + 1, B, NZ),
        pltpu.SemaphoreType.DMA((2,)),
        pltpu.SemaphoreType.DMA((7,)),
        pltpu.SemaphoreType.DMA((7,)),
    ]
    return pl.pallas_call(
        kernel,
        out_shape=jax.ShapeDtypeStruct((B, B, NZ), jnp.float32),
        in_specs=[pl.BlockSpec(memory_space=pltpu.HBM)] * 2,
        out_specs=pl.BlockSpec(memory_space=pltpu.VMEM),
        scratch_shapes=scratch,
        compiler_params=pltpu.CompilerParams(
            collective_id=0, has_side_effects=True, vmem_limit_bytes=55040 * 1024
        ),
    )(warmth, factor)


def solution(mesh):
    return jax.shard_map(
        shards,
        mesh=mesh,
        in_specs=(P("row", "col", None), P("row", "col", None)),
        out_specs=P("row", "col", None),
        check_vma=False,
    )
```
